32 devices in a mesh: grp: 2 (over y), win: 4 (over z), uly: 4 (over x, core).
Axes of the slice: x: 2, y: 2, z: 4, core: 2. Of those that a mesh axis runs over, the one named last changes fastest.
Arguments:
- query_rows: bfloat16 [8, 16, 64, 5120], P(('grp', 'win'), None, 'uly'), parts along dimension 0, may hold values from -140 to 140
- key_rows: bfloat16 [8, 16, 64, 5120], P(('grp', 'win'), None, 'uly'), parts along dimension 0, may hold values from -140 to 140
- value_rows: bfloat16 [8, 16, 64, 5120], P(('grp', 'win'), None, 'uly'), parts along dimension 0, may hold values from -6 to 6
- query_gain: float32 [5120], replicated, may hold values from 0.25 to 1.75
- key_gain: float32 [5120], replicated, may hold values from 0.25 to 1.75
- window_start: int32 [8], P('grp'), parts along dimension 0, may hold values from 0 to 40, as said below
- owner_of_phase: int32 [8], P('grp'), parts along dimension 0, may hold values from 0 to 3, each once
- blend_weight: int32 [8, 16], P('grp'), parts along dimension 0, may hold values from 1 to 8
Outputs:
- owned_frames: bfloat16 [96, 64, 5120], P(('grp', 'win'), 'uly'), parts along dimension 0
- next_windows: bfloat16 [8, 16, 64, 5120], P(('grp', 'win'), None, 'uly'), parts along dimension 0
The draws below stay inside these ranges and needn't reach their ends.
There are 2 independent parts, one for each index of `grp`. The reference program is written for one: setup_inputs(seed, part) draws one part's arguments, and reference() takes and returns one part's arrays. A program takes and returns all parts, laid end to end along the dimension named above; an argument that names none is the same for every part. Nothing has to cross between parts.
Inputs may be any that keep to these rules, and one draw needn't show every extreme that they name: `window_start`: window w starts at frame w * 12 plus an offset of 0 to 4; in some pair of consecutive windows (the last one followed by the first counts as consecutive) the first offset is 4 and the second 0. `owner_of_phase`: a permutation.
All inputs are finite; a program needn't handle non-finite values.
Results may differ from the reference program's by a relative error of at most 0.0015.
The reference program's roundings to bfloat16 on the way count: a program that leaves them out, or rounds other values in their place, can miss the bound.
Values may be sent and summed in bfloat16 or wider, within the bound.
No kernel may reach another device: no remote copies, remote signals or barrier semaphores. Data moves between devices by JAX's collectives and lax.ppermute only.
A program may use at most 128 MiB of HBM per device.

```python
import math
import jax
import jax.numpy as jnp
from jax import lax

D = 5120
HEADS = 40
HD = 128
P_SIZE = 64
WF = 16
FR = 12
SHIFT = 6
NW = 4
FRAMES = 48


def shared_layout(key):
    column_scale = jnp.exp(jax.random.uniform(jax.random.fold_in(key, 11), (D,), jnp.float32) * math.log(10.0))
    return column_scale


def draw_query_rows(key, part):
    column_scale = shared_layout(key)
    own_key = jax.random.fold_in(key, 21)
    drawn = jnp.clip(jax.random.normal(own_key, (NW, WF, P_SIZE, D), jnp.float32), -6.0, 6.0) * column_scale
    return drawn.astype(jnp.bfloat16)


def draw_key_rows(key, part):
    column_scale = shared_layout(key)
    own_key = jax.random.fold_in(key, 31)
    drawn = jnp.clip(jax.random.normal(own_key, (NW, WF, P_SIZE, D), jnp.float32), -6.0, 6.0) * column_scale
    return drawn.astype(jnp.bfloat16)


def draw_window_start(key, part):
    offsets = jax.random.randint(jax.random.fold_in(key, 41), (NW,), 0, WF - FR + 1)
    chosen = jax.random.randint(jax.random.fold_in(key, 42), (), 0, NW)
    window_index = jnp.arange(NW)
    offsets = jnp.where(window_index == chosen, WF - FR, offsets)
    offsets = jnp.where(window_index == (chosen + 1) % NW, 0, offsets)
    return (window_index * FR + offsets).astype(jnp.int32)


def plant(entries, rng, least, high):
    extent = entries.shape
    place = [jax.random.randint(jax.random.fold_in(rng, axis), (), 0, extent[axis]) for axis in range(len(extent))]
    entries = entries.at[tuple(place)].set(least)
    longest = extent.index(max(extent))
    place[longest] = (place[longest] + 1) % extent[longest]
    return entries.at[tuple(place)].set(high)


def levels(rng, extent, shards, least, largest):
    def one(dim, parts):
        draws = jax.random.uniform(jax.random.fold_in(jax.random.fold_in(rng, 6), dim), (parts,), jnp.float32, least / len(shards), largest / len(shards))
        return jnp.repeat(jnp.exp(draws), extent[dim] // parts).reshape((-1,) + (1,) * (len(extent) - dim - 1))

    loudness = one(*shards[0])
    for cut in shards[1:]:
        loudness = loudness * one(*cut)
    return loudness


def noise(stream_key, shape, scale, reach, pieces=(), held_as=jnp.bfloat16):
    entries = scale * jax.random.normal(stream_key, shape, jnp.float32)
    if pieces:
        entries = entries * levels(stream_key, shape, pieces, -0.22, 0.18)
    return jnp.clip(entries, -reach, reach).astype(held_as)


def setup_inputs(seed: int = 0, part: int = 0) -> dict:
    key_list = jax.random.split(jax.random.key(seed), 9)
    own_keys = jax.random.split(jax.random.fold_in(key_list[8], part), 9)
    query_rows = draw_query_rows(jax.random.fold_in(jax.random.fold_in(key_list[8], part), 71), part)
    key_rows = draw_key_rows(jax.random.fold_in(jax.random.fold_in(key_list[8], part), 71), part)
    value_rows = noise(own_keys[2], (NW, WF, P_SIZE, D), 1.0, 6.0, ((0, 4), (2, 4)))
    query_gain = jnp.clip(1.0 + 0.15 * jax.random.normal(key_list[3], (D,), jnp.float32), 0.25, 1.75)
    key_gain = jnp.clip(1.0 + 0.15 * jax.random.normal(key_list[4], (D,), jnp.float32), 0.25, 1.75)
    window_start = draw_window_start(jax.random.fold_in(jax.random.fold_in(key_list[8], part), 71), part)
    owner_of_phase = jax.random.permutation(own_keys[6], NW).astype(jnp.int32)
    blend_weight = plant(jax.random.randint(own_keys[7], (NW, WF), 1, 9), jax.random.fold_in(own_keys[7], 1), 1, 8).astype(jnp.int32)
    return dict(query_rows=query_rows, key_rows=key_rows, value_rows=value_rows, query_gain=query_gain, key_gain=key_gain, window_start=window_start, owner_of_phase=owner_of_phase, blend_weight=blend_weight)


def normalize(row_block, gain_vector):
    floats = row_block.astype(jnp.float32)
    mean_square = lax.optimization_barrier(jnp.mean(floats * floats, axis=-1, keepdims=True))
    return (floats * lax.rsqrt(mean_square + 1e-06) * gain_vector).astype(jnp.bfloat16)

def head_attention(operands):
    query_head, key_head, value_head = operands
    scores = jnp.dot(query_head, key_head.T, preferred_element_type=jnp.float32) * (1.0 / math.sqrt(query_head.shape[-1]))
    row_max = lax.optimization_barrier(jnp.max(scores, axis=-1, keepdims=True))
    exponent = jnp.exp(scores - row_max)
    weights = (exponent / lax.optimization_barrier(jnp.sum(exponent, axis=-1, keepdims=True))).astype(jnp.bfloat16)
    return jnp.dot(weights, value_head, preferred_element_type=jnp.float32).astype(jnp.bfloat16)

def reference(query_rows, key_rows, value_rows, query_gain, key_gain, window_start, owner_of_phase, blend_weight):
    token_count = WF * P_SIZE

    def split_heads(tensor):
        return jnp.moveaxis(tensor.reshape(token_count, HEADS, HD), 1, 0)

    def window_attention(operands):
        query_win, key_win, value_win = operands
        result = lax.map(head_attention, (split_heads(normalize(query_win, query_gain)), split_heads(normalize(key_win, key_gain)), split_heads(value_win)))
        return jnp.moveaxis(result, 0, 1).reshape(WF, P_SIZE, D)
    window_out = lax.map(window_attention, (query_rows, key_rows, value_rows))
    frame_range = jnp.arange(WF, dtype=jnp.int32)
    frame_of = ((window_start[:, None] + frame_range[None, :]) % FRAMES).reshape(-1).astype(jnp.int32)
    weight_float = blend_weight.astype(jnp.float32)
    terms = (weight_float[:, :, None, None] * window_out.astype(jnp.float32)).reshape(NW * WF, P_SIZE, D)
    numerator = jnp.zeros((FRAMES, P_SIZE, D), jnp.float32).at[frame_of].add(terms)
    denominator = jnp.zeros((FRAMES,), jnp.float32).at[frame_of].add(weight_float.reshape(-1))
    blended = (numerator / denominator[:, None, None]).astype(jnp.bfloat16)
    phase_range = jnp.arange(NW, dtype=jnp.int32)
    inverse = jnp.zeros((NW,), jnp.int32).at[owner_of_phase].set(phase_range)
    owned_index = (jnp.arange(FR, dtype=jnp.int32)[None, :] * NW + inverse[:, None]).reshape(-1).astype(jnp.int32)
    owned_frames = blended[owned_index]
    next_index = ((window_start[:, None] + SHIFT + frame_range[None, :]) % FRAMES).reshape(-1).astype(jnp.int32)
    next_windows = blended[next_index].reshape(NW, WF, P_SIZE, D)
    return (owned_frames, next_windows)
```

```python
import functools
import math

import jax
import jax.numpy as jnp
from jax import lax
from jax.experimental import pallas as pl
from jax.experimental.pallas import tpu as pltpu
from jax.sharding import PartitionSpec as P

HEADS = 40
WF = 16
FR = 12
MARGIN = WF - FR
SHIFT = FR // 2
NEXT = SHIFT + MARGIN
CHUNK_HEADS = (8, 8, 8, 8, 8)
VMEM_LIMIT = 48 * 1024 * 1024


def params():
    return pltpu.CompilerParams(vmem_limit_bytes=VMEM_LIMIT)


def normalized(rows, gain):
    floats = rows.astype(jnp.float32)
    mean_square = jnp.mean(floats * floats, axis=-1, keepdims=True)
    return (floats * lax.rsqrt(mean_square + 1e-06) * gain).astype(jnp.bfloat16)


def query_kernel(query_ref, gain_ref, out_ref):
    out_ref[...] = normalized(query_ref[...], gain_ref[...])


def normalize_queries(rows, gain, frames_per_step=4):
    frames, tokens, features = rows.shape
    block = (frames_per_step, tokens, features)
    return pl.pallas_call(
        query_kernel,
        grid=(frames // frames_per_step,),
        in_specs=[
            pl.BlockSpec(block, lambda i: (i, 0, 0)),
            pl.BlockSpec((1, 1, features), lambda i: (0, 0, 0)),
        ],
        out_specs=pl.BlockSpec(block, lambda i: (i, 0, 0)),
        out_shape=jax.ShapeDtypeStruct(rows.shape, jnp.bfloat16),
        compiler_params=params(),
        cost_estimate=pl.CostEstimate(
            flops=rows.size * 6, bytes_accessed=rows.size * 4, transcendentals=0
        ),
        name="query_norm",
    )(rows, gain)


def pack_kernel(key_ref, value_ref, gain_ref, *out_refs):
    keys = normalized(key_ref[...], gain_ref[...])
    offset = 0
    for out_ref in out_refs:
        width = out_ref.shape[-1]
        out_ref[0] = keys[:, :, offset : offset + width]
        out_ref[1] = value_ref[:, :, offset : offset + width]
        offset += width


def pack_keys_values(key_rows, value_rows, gain, widths, frames_per_step=4):
    frames, tokens, features = key_rows.shape
    block = (frames_per_step, tokens, features)
    return pl.pallas_call(
        pack_kernel,
        grid=(frames // frames_per_step,),
        in_specs=[
            pl.BlockSpec(block, lambda i: (i, 0, 0)),
            pl.BlockSpec(block, lambda i: (i, 0, 0)),
            pl.BlockSpec((1, 1, features), lambda i: (0, 0, 0)),
        ],
        out_specs=[
            pl.BlockSpec((2, frames_per_step, tokens, width), lambda i: (0, i, 0, 0))
            for width in widths
        ],
        out_shape=[
            jax.ShapeDtypeStruct((2, frames, tokens, width), jnp.bfloat16) for width in widths
        ],
        compiler_params=params(),
        cost_estimate=pl.CostEstimate(
            flops=key_rows.size * 6, bytes_accessed=key_rows.size * 8, transcendentals=0
        ),
        name="key_norm_pack",
    )(key_rows, value_rows, gain)


def attention_kernel(head_size, query_ref, *refs):
    sources, (out_ref, first_ref, last_ref) = refs[:-3], refs[-3:]
    frames, tokens, width = query_ref.shape
    rows = frames * tokens
    factor = math.log2(math.e) / math.sqrt(head_size)
    contract = (((1,), (1,)), ((), ()))
    for start in range(0, width, head_size):
        columns = slice(start, start + head_size)
        query = query_ref[:, :, columns].reshape(rows, head_size)
        scores = [
            lax.dot_general(
                query,
                source[0, :, :, columns].reshape(rows, head_size),
                contract,
                preferred_element_type=jnp.float32,
            )
            for source in sources
        ]
        row_max = functools.reduce(jnp.maximum, scores)
        row_max = jnp.max(row_max, axis=-1, keepdims=True)
        exponents = [jnp.exp2((score - row_max) * factor) for score in scores]
        total = jnp.sum(functools.reduce(jnp.add, exponents), axis=-1, keepdims=True)
        inverse = 1.0 / total
        result = jnp.zeros((rows, head_size), jnp.float32)
        for exponent, source in zip(exponents, sources):
            weights = (exponent * inverse).astype(jnp.bfloat16)
            result += jnp.dot(
                weights,
                source[1, :, :, columns].reshape(rows, head_size),
                preferred_element_type=jnp.float32,
            )
        result = result.astype(jnp.bfloat16).reshape(frames, tokens, head_size)
        out_ref[:, :, columns] = result
        first_ref[:, :, columns] = result[:MARGIN]
        last_ref[:, :, columns] = result[frames - MARGIN :]


def attend(queries, sources, base, width, head_size, block_width):
    frames, tokens, _ = queries.shape
    base_block = base // block_width
    rows = frames * tokens
    heads = width // head_size
    keys = rows * len(sources)

    def spec(count):
        return pl.BlockSpec((count, tokens, block_width), lambda i: (0, 0, i))

    return pl.pallas_call(
        functools.partial(attention_kernel, head_size),
        grid=(width // block_width,),
        in_specs=[
            pl.BlockSpec((frames, tokens, block_width), lambda i: (0, 0, base_block + i))
        ]
        + [
            pl.BlockSpec((2, frames, tokens, block_width), lambda i: (0, 0, 0, i))
            for _ in sources
        ],
        out_specs=[spec(frames), spec(MARGIN), spec(MARGIN)],
        out_shape=[
            jax.ShapeDtypeStruct((count, tokens, width), jnp.bfloat16)
            for count in (frames, MARGIN, MARGIN)
        ],
        compiler_params=params(),
        cost_estimate=pl.CostEstimate(
            flops=4 * rows * keys * width,
            bytes_accessed=rows * width * 4 * (1 + len(sources)),
            transcendentals=rows * keys * heads,
        ),
        name="attention",
    )(queries, *sources)


def phase_of(owner_ref, wanted, windows):
    phase = jnp.int32(0)
    for index in range(windows):
        phase = jnp.where(owner_ref[index] == wanted, index, phase)
    return phase


def first_owned(phase, windows):
    return lax.rem(phase + (windows - 1) * MARGIN, windows)


def extra_owned(windows):
    return [i for i in range(FR // windows) if windows * (i + 1) > NEXT]


def blend_kernel(
    windows, place_ref, start_ref, owner_ref, weight_ref, out_ref, before_ref, after_ref, home_ref, *sent_refs
):
    here = place_ref[0]
    before = lax.rem(here + windows - 1, windows)
    after = lax.rem(here + 1, windows)
    offset = start_ref[here] - here * FR
    offset_before = start_ref[before] - before * FR
    offset_after = start_ref[after] - after * FR
    for frame in range(FR):
        place = frame + MARGIN - offset
        weight = weight_ref[here, place].astype(jnp.float32)
        numerator = out_ref[place].astype(jnp.float32) * weight
        denominator = weight
        if frame < MARGIN:
            valid = frame < offset_before
            slot = jnp.minimum(frame + MARGIN - offset_before, MARGIN - 1)
            weight = jnp.where(valid, weight_ref[before, slot + FR], 0).astype(jnp.float32)
            numerator += before_ref[slot].astype(jnp.float32) * weight
            denominator += weight
        if frame >= FR - MARGIN:
            slot = frame - (FR - MARGIN) - offset_after
            valid = slot >= 0
            slot = jnp.maximum(slot, 0)
            weight = jnp.where(valid, weight_ref[after, slot], 0).astype(jnp.float32)
            numerator += after_ref[slot].astype(jnp.float32) * weight
            denominator += weight
        home_ref[frame] = (numerator / denominator).astype(jnp.bfloat16)
    for step, sent_ref in enumerate(sent_refs, 1):
        target = lax.rem(here + step, windows)
        first = first_owned(phase_of(owner_ref, target, windows), windows)
        if step < windows - 1:
            for index in range(FR // windows):
                sent_ref[index] = home_ref[first + index * windows]
        else:
            sent_ref[:NEXT] = home_ref[:NEXT]
            for slot, index in enumerate(extra_owned(windows)):
                sent_ref[NEXT + slot] = home_ref[first + index * windows]


def blend(tables, out, before, after, windows, block_width):
    _, tokens, width = out.shape
    counts = [FR] + [FR // windows] * (windows - 2) + [NEXT + len(extra_owned(windows))]

    def spec(count):
        return pl.BlockSpec((count, tokens, block_width), lambda i: (0, 0, i))

    return pl.pallas_call(
        functools.partial(blend_kernel, windows),
        grid=(width // block_width,),
        in_specs=[pl.BlockSpec(memory_space=pltpu.SMEM) for _ in tables]
        + [spec(out.shape[0]), spec(MARGIN), spec(MARGIN)],
        out_specs=[spec(count) for count in counts],
        out_shape=[jax.ShapeDtypeStruct((count, tokens, width), jnp.bfloat16) for count in counts],
        compiler_params=params(),
        cost_estimate=pl.CostEstimate(
            flops=tokens * width * FR * 8,
            bytes_accessed=tokens * width * 2 * (WF + 2 * MARGIN + sum(counts)),
            transcendentals=0,
        ),
        name="blend",
    )(*tables, out, before, after)


def place_kernel(windows, place_ref, start_ref, owner_ref, weight_ref, home_ref, *refs):
    received, (owned_ref, next_ref) = refs[: windows - 1], refs[-2:]
    here = place_ref[0]
    phase = phase_of(owner_ref, here, windows)
    first = first_owned(phase, windows)
    slot_base = (first + MARGIN) // windows
    count = FR // windows
    extra = extra_owned(windows)
    for step in range(windows):
        source = lax.rem(here + windows - step, windows)
        for index in range(count):
            slot = lax.rem(source * count + slot_base + index, FR)
            if step == 0:
                row = home_ref[first + index * windows]
            elif step < windows - 1:
                row = received[step - 1][index]
            elif index in extra:
                row = received[step - 1][NEXT + extra.index(index)]
            else:
                row = received[step - 1][first + index * windows]
            owned_ref[slot] = row
    offset = start_ref[here] - here * FR + SHIFT - MARGIN
    from_after = received[-1]
    for frame in range(WF):
        wanted = offset + frame
        if frame + MARGIN + SHIFT - MARGIN < FR:
            next_ref[frame] = home_ref[wanted]
        elif frame + SHIFT - MARGIN >= FR:
            next_ref[frame] = from_after[wanted - FR]
        else:
            inside = wanted < FR
            next_ref[frame] = jnp.where(
                inside,
                home_ref[jnp.minimum(wanted, FR - 1)],
                from_after[jnp.maximum(wanted - FR, 0)],
            )


def place(tables, home, received, base, features, targets, windows, block_width):
    _, tokens, width = home.shape
    base_block = base // block_width

    def spec(count):
        return pl.BlockSpec((count, tokens, block_width), lambda i: (0, 0, i))

    def out_spec(count):
        return pl.BlockSpec((count, tokens, block_width), lambda i: (0, 0, base_block + i))

    operands = (*tables, home, *received)
    return pl.pallas_call(
        functools.partial(place_kernel, windows),
        grid=(width // block_width,),
        in_specs=[pl.BlockSpec(memory_space=pltpu.SMEM) for _ in tables]
        + [spec(array.shape[0]) for array in (home, *received)]
        + [pl.BlockSpec(memory_space=pl.ANY) for _ in targets],
        out_specs=[out_spec(FR), out_spec(WF)],
        out_shape=[
            jax.ShapeDtypeStruct((count, tokens, features), jnp.bfloat16) for count in (FR, WF)
        ],
        input_output_aliases={len(operands) + i: i for i in range(len(targets))},
        compiler_params=params(),
        cost_estimate=pl.CostEstimate(
            flops=0, bytes_accessed=tokens * width * 4 * (FR + WF), transcendentals=0
        ),
        name="place",
    )(*operands, *targets)


def exchange(array, axis, bit):
    return lax.ppermute(array, axis, [(i, i ^ bit) for i in range(lax.axis_size(axis))])


def shift(array, axis, step):
    count = lax.axis_size(axis)
    return lax.ppermute(array, axis, [(i, (i + step) % count) for i in range(count)])


def gather_blocks(array, axis):
    count = lax.axis_size(axis)
    if count & (count - 1):
        gathered = lax.all_gather(array, axis)
        return [gathered[i] for i in range(count)]
    blocks = [array]
    bit = count // 2
    while bit:
        blocks += [exchange(block, axis, bit) for block in blocks]
        bit //= 2
    return blocks


def table_lookup(table_row, wanted, length):
    entries = jnp.arange(length, dtype=jnp.int32)
    return jnp.sum(jnp.where(wanted[..., None] == entries, table_row, 0), axis=-1)


def send_owners(frame_rows, inverse, my_start, windows, capacity):
    slot_index = jnp.arange(capacity, dtype=jnp.int32)
    position_in = (inverse[:, None] - my_start) % windows + slot_index[None, :] * windows
    is_valid = (position_in < WF).reshape(-1)
    picked = jnp.take(frame_rows, jnp.minimum(position_in, WF - 1).reshape(-1), axis=0)
    picked = jnp.where(is_valid[:, None, None], picked, jnp.zeros_like(picked))
    packed = picked.reshape(windows, capacity, frame_rows.shape[1], frame_rows.shape[2])
    return lax.all_to_all(packed, "win", split_axis=0, concat_axis=0, tiled=True)


def combine_owned(received, window_start, blend_weight, my_phase, windows, frames_total, capacity):
    slot_index = jnp.arange(capacity, dtype=jnp.int32)
    source_pos = (my_phase - window_start[:, None]) % windows + slot_index[None, :] * windows
    arrived = source_pos < WF
    slot_at = (window_start[:, None] + source_pos) % frames_total // windows
    factor = table_lookup(blend_weight[:, None, :], source_pos, WF)
    owned_range = jnp.arange(FR, dtype=jnp.int32)
    mixing = jnp.where(
        (slot_at[None] == owned_range[:, None, None]) & arrived[None], factor[None], 0
    )
    mixing = mixing.reshape(FR, windows * capacity).astype(jnp.float32)
    numerator = jnp.dot(
        mixing.astype(jnp.bfloat16),
        received.reshape(windows * capacity, -1),
        preferred_element_type=jnp.float32,
    )
    denominator = jnp.sum(mixing, axis=1)
    owned = (numerator / denominator[:, None]).astype(jnp.bfloat16)
    return owned.reshape(FR, received.shape[2], received.shape[3])


def blend_by_owners(own_out, window_start, owner_of_phase, blend_weight):
    windows = lax.axis_size("win")
    position = lax.axis_index("win")
    frames_total = FR * windows
    capacity = (WF + windows - 1) // windows
    _, local_tokens, feature_count = own_out.shape
    phases = jnp.arange(windows, dtype=jnp.int32)
    inverse = jnp.sum(
        jnp.where(owner_of_phase[None, :] == phases[:, None], phases[None, :], 0), axis=1
    )
    my_start = window_start[position]
    my_phase = inverse[position]
    frame_range = jnp.arange(WF, dtype=jnp.int32)
    received = send_owners(own_out, inverse, my_start, windows, capacity)
    owned = combine_owned(
        received, window_start, blend_weight, my_phase, windows, frames_total, capacity
    )
    slot_index = jnp.arange(capacity, dtype=jnp.int32)
    target_pos = (my_phase - window_start[:, None] - SHIFT) % windows + slot_index[
        None, :
    ] * windows
    target_valid = (target_pos < WF).reshape(-1)
    target_slot = (
        (window_start[:, None] + SHIFT + target_pos) % frames_total // windows
    ).reshape(-1)
    outgoing = jnp.take(owned, target_slot, axis=0)
    outgoing = jnp.where(target_valid[:, None, None], outgoing, jnp.zeros_like(outgoing))
    outgoing = outgoing.reshape(windows, capacity, local_tokens, feature_count)
    returned = lax.all_to_all(outgoing, "win", split_axis=0, concat_axis=0, tiled=True)
    needed_phase = (my_start + SHIFT + frame_range) % windows
    source_owner = table_lookup(owner_of_phase[None, :], needed_phase, windows)
    flat_index = source_owner * capacity + frame_range // windows
    next_rows = jnp.take(
        returned.reshape(windows * capacity, local_tokens, feature_count), flat_index, axis=0
    )
    return owned, next_rows


def per_device(
    query_rows,
    key_rows,
    value_rows,
    query_gain,
    key_gain,
    window_start,
    owner_of_phase,
    blend_weight,
):
    windows = lax.axis_size("win")
    features = query_rows.shape[-1]
    head_size = features // HEADS
    block_width = 2 * head_size
    widths = [heads * head_size for heads in CHUNK_HEADS]
    packed = pack_keys_values(
        key_rows[0], value_rows[0], key_gain.reshape(1, 1, features), widths
    )
    queries = normalize_queries(query_rows[0], query_gain.reshape(1, 1, features))
    direct = windows >= 3 and FR % windows == 0
    tables = (
        lax.axis_index("win").astype(jnp.int32).reshape(1),
        window_start,
        owner_of_phase,
        blend_weight,
    )
    targets = ()
    whole = []
    base = 0
    for width, own in zip(widths, packed):
        out, first, last = attend(
            queries, gather_blocks(own, "uly"), base, width, head_size, block_width
        )
        if direct:
            before = shift(last, "win", 1)
            after = shift(first, "win", -1)
            home, *sent = blend(tables, out, before, after, windows, block_width)
            received = [shift(array, "win", step) for step, array in enumerate(sent, 1)]
            targets = place(tables, home, received, base, features, targets, windows, block_width)
        else:
            whole.append(out)
        base += width
    if direct:
        owned, next_rows = targets
    else:
        owned, next_rows = blend_by_owners(
            jnp.concatenate(whole, axis=-1), window_start, owner_of_phase, blend_weight
        )
    return (owned, next_rows[None])


def solution(mesh):
    placed = (
        P(("grp", "win"), None, "uly", None),
        P(("grp", "win"), None, "uly", None),
        P(("grp", "win"), None, "uly", None),
        P(),
        P(),
        P("grp"),
        P("grp"),
        P("grp", None),
    )
    return jax.shard_map(
        per_device,
        mesh=mesh,
        in_specs=placed,
        out_specs=(P(("grp", "win"), "uly", None), P(("grp", "win"), None, "uly", None)),
        check_vma=False,
    )
```

```python
import functools
import math

import jax
import jax.numpy as jnp
from jax import lax
from jax.experimental import pallas as pl
from jax.experimental.pallas import tpu as pltpu
from jax.sharding import PartitionSpec as P

HEADS = 40
WF = 16
FR = 12
MARGIN = WF - FR
SHIFT = FR // 2
HOME_BASE = 2 * MARGIN
FROM_BEFORE = HOME_BASE - SHIFT
FROM_AFTER = SHIFT + WF + MARGIN - HOME_BASE - FR
NEAR = 2
CHUNKS = (2, 4, 4, 4, 4, 2)
STEP_HEADS = 2
VMEM_LIMIT = 64 * 1024 * 1024


def params():
    return pltpu.CompilerParams(vmem_limit_bytes=VMEM_LIMIT)


def like(*shape):
    return jax.ShapeDtypeStruct(shape, jnp.bfloat16)


FILLER = pl.CostEstimate(flops=10**10, bytes_accessed=0, transcendentals=0)
NO_COST = pl.CostEstimate(flops=0, bytes_accessed=0, transcendentals=0)
SMEM = pl.BlockSpec(memory_space=pltpu.SMEM)


def normalized(rows, gain):
    floats = rows.astype(jnp.float32)
    mean_square = jnp.mean(floats * floats, axis=-1, keepdims=True)
    return (floats * lax.rsqrt(mean_square + 1e-06) * gain).astype(jnp.bfloat16)


def split_heads(near, rows, gain, counts, plain=(), frames_per_step=4):
    frames, tokens, features = rows.shape
    head_size = features // HEADS
    kinds = (2,) * len(plain)

    def kernel(near_ref, rows_ref, gain_ref, *refs):
        scratch = refs[-1]
        plain_refs, out_refs = refs[: len(plain)], refs[len(plain) : -1]
        heads = HEADS // NEAR
        scratch[...] = normalized(rows_ref[...], gain_ref[...])
        here = near_ref[0]

        def put(out_ref, slot, half, head):
            column = pl.multiple_of((half * heads + head) * head_size, head_size)
            columns = pl.ds(column, head_size)
            if plain:
                out_ref[slot, 0] = scratch[:, :, columns]
                out_ref[slot, 1] = plain_refs[0][:, :, columns]
            else:
                out_ref[slot] = scratch[:, :, columns]

        for head in range(heads):
            put(out_refs[0], head, here, head)
        head = 0
        for out_ref in out_refs[1:]:
            for slot in range(out_ref.shape[0]):
                put(out_ref, slot, NEAR - 1 - here, head)
                head += 1

    block = pl.BlockSpec((frames_per_step, tokens, features), lambda i: (i, 0, 0))

    def out_spec(count):
        zeros = (0,) * (1 + len(kinds))
        return pl.BlockSpec(
            (count, *kinds, frames_per_step, tokens, head_size), lambda i: (*zeros, i, 0, 0)
        )

    return pl.pallas_call(
        kernel,
        grid=(frames // frames_per_step,),
        in_specs=[SMEM, block, pl.BlockSpec((1, 1, features), lambda i: (0, 0, 0))]
        + [block for _ in plain],
        out_specs=[out_spec(count) for count in (sum(counts), *counts)],
        out_shape=[
            like(count, *kinds, frames, tokens, head_size) for count in (sum(counts), *counts)
        ],
        scratch_shapes=[pltpu.VMEM((frames_per_step, tokens, features), jnp.bfloat16)],
        compiler_params=params(),
        cost_estimate=FILLER,
        name="norm_split",
    )(near, rows, gain, *plain)


def join_halves(own, base, other, counts):
    _, kinds, frames, tokens, head_size = own.shape
    bases = [sum(counts[:i]) for i in range(len(counts))]

    def out_spec(first, count):
        return pl.BlockSpec(
            (STEP_HEADS, kinds, NEAR, frames, tokens, head_size),
            lambda i: (jnp.clip(i - first // STEP_HEADS, 0, count // STEP_HEADS - 1),) + (0,) * 5,
        )

    def kernel(own_ref, other_ref, *out_refs):
        step = pl.program_id(0) * STEP_HEADS
        for out_ref, first, count in zip(out_refs, bases, counts):

            @pl.when((step >= first) & (step < first + count))
            def _():
                out_ref[:, :, 0] = own_ref[...]
                out_ref[:, :, 1] = other_ref[...]

    block = (STEP_HEADS, kinds, frames, tokens, head_size)
    return pl.pallas_call(
        kernel,
        grid=(sum(counts) // STEP_HEADS,),
        in_specs=[
            pl.BlockSpec(block, lambda i: (base // STEP_HEADS + i, 0, 0, 0, 0)),
            pl.BlockSpec(block, lambda i: (i, 0, 0, 0, 0)),
        ],
        out_specs=[out_spec(first, count) for first, count in zip(bases, counts)],
        out_shape=[
            like(count, kinds, NEAR, frames, tokens, head_size) for count in counts
        ],
        compiler_params=params(),
        cost_estimate=FILLER,
        name="join_halves",
    )(own, other)


def attention_body(tables, in_refs, out_refs, left_ref, left_base):
    (out_ref,) = out_refs
    query_refs, sources = in_refs[:NEAR], in_refs[NEAR:]
    _, frames, tokens, head_size = query_refs[0].shape
    rows = frames * tokens
    factor = math.log2(math.e) / math.sqrt(head_size)
    contract = (((1,), (1,)), ((), ()))
    step = pl.program_id(0)
    for half in range(NEAR):
        query = query_refs[half][0].reshape(rows, head_size)
        scores = [
            lax.dot_general(
                query,
                source[0, 0].reshape(NEAR * rows, head_size),
                contract,
                preferred_element_type=jnp.float32,
            )
            for source in sources
        ]
        row_max = functools.reduce(jnp.maximum, scores)
        row_max = jnp.max(row_max, axis=-1, keepdims=True)
        exponents = [jnp.exp2((score - row_max) * factor) for score in scores]
        total = jnp.sum(functools.reduce(jnp.add, exponents), axis=-1, keepdims=True)
        inverse = 1.0 / total
        result = jnp.zeros((rows, head_size), jnp.float32)
        for exponent, source in zip(exponents, sources):
            weights = (exponent * inverse).astype(jnp.bfloat16)
            result += jnp.dot(
                weights,
                source[0, 1].reshape(NEAR * rows, head_size),
                preferred_element_type=jnp.float32,
            )
        result = result.astype(jnp.bfloat16).reshape(frames, tokens, head_size)
        out_ref[0, half] = result
        left_ref[left_base + step, half] = result[:HOME_BASE]


def phase_of(owner_ref, wanted, windows):
    phase = jnp.int32(0)
    for index in range(windows):
        phase = jnp.where(owner_ref[index] == wanted, index, phase)
    return phase


def first_owned(phase, windows):
    return lax.rem(phase + (windows - 1) * HOME_BASE, windows)


def extra_owned(windows):
    return [i for i in range(FR // windows) if windows * (i + 1) > FROM_AFTER]


def left_count(windows):
    return FROM_AFTER + len(extra_owned(windows))


def blend_body(windows, tables, in_refs, out_refs, left_ref, left_base):
    place_ref, start_ref, owner_ref, weight_ref, _ = tables
    out_ref, after_ref = in_refs
    home_ref, *sent_refs = out_refs
    here = place_ref[0]
    after = lax.rem(here + 1, windows)
    offset = start_ref[here] - here * FR
    offset_after = start_ref[after] - after * FR
    step = pl.program_id(0)
    for frame in range(FR):
        place = frame + HOME_BASE - offset
        if frame + HOME_BASE < WF:
            weight = weight_ref[here, place].astype(jnp.float32)
        else:
            valid = place < WF
            place = jnp.minimum(place, WF - 1)
            weight = jnp.where(valid, weight_ref[here, place], 0).astype(jnp.float32)
        numerator = out_ref[0, :, place].astype(jnp.float32) * weight
        denominator = weight
        if frame + HOME_BASE >= FR:
            slot = frame + HOME_BASE - FR - offset_after
            valid = slot >= 0
            slot = jnp.maximum(slot, 0)
            weight = jnp.where(valid, weight_ref[after, slot], 0).astype(jnp.float32)
            numerator += after_ref[0, :, slot].astype(jnp.float32) * weight
            denominator += weight
        home_ref[0, :, frame] = (numerator / denominator).astype(jnp.bfloat16)
    for distance in range(1, windows):
        target = lax.rem(here + distance, windows)
        first = first_owned(phase_of(owner_ref, target, windows), windows)
        if distance == windows - 1:
            left_ref[left_base + step, :, :FROM_AFTER] = home_ref[0, :, :FROM_AFTER]
            for slot, index in enumerate(extra_owned(windows)):
                left_ref[left_base + step, :, FROM_AFTER + slot] = home_ref[
                    0, :, first + index * windows
                ]
            continue
        sent_ref = sent_refs[distance - 1]
        for index in range(FR // windows):
            sent_ref[0, :, index] = home_ref[0, :, first + index * windows]
        if distance == 1:
            sent_ref[0, :, FR // windows :] = home_ref[0, :, FR - FROM_BEFORE :]


def place_body(windows, tables, in_refs, out_refs):
    place_ref, start_ref, owner_ref = tables[:3]
    home_ref, *received = in_refs
    owned_ref, next_ref, other_ref = out_refs
    here = place_ref[0]
    first = first_owned(phase_of(owner_ref, here, windows), windows)
    slot_base = (first + HOME_BASE) // windows
    count = FR // windows
    extra = extra_owned(windows)
    heads, _, _, _, head_size = home_ref.shape
    offset = start_ref[here] - here * FR + SHIFT - HOME_BASE
    from_before, from_after = received[0], received[-1]
    for head in range(heads):
        columns = slice(head * head_size, (head + 1) * head_size)
        for distance in range(windows):
            source = lax.rem(here + windows - distance, windows)
            for index in range(count):
                slot = lax.rem(source * count + slot_base + index, FR)
                if distance == 0:
                    row = home_ref[head, :, first + index * windows]
                elif distance < windows - 1:
                    row = received[distance - 1][head, :, index]
                elif index in extra:
                    row = received[distance - 1][head, :, FROM_AFTER + extra.index(index)]
                else:
                    row = received[distance - 1][head, :, first + index * windows]
                owned_ref[slot, :, columns] = row[0]
                other_ref[slot, :, columns] = row[1]
        for frame in range(WF):
            wanted = offset + frame
            row = home_ref[head, :, jnp.clip(wanted, 0, FR - 1)]
            if frame < FROM_BEFORE:
                slot = jnp.clip(wanted + FROM_BEFORE, 0, FROM_BEFORE - 1)
                row = jnp.where(wanted < 0, from_before[head, :, count + slot], row)
            if frame + MARGIN + SHIFT - HOME_BASE >= FR:
                slot = jnp.clip(wanted - FR, 0, FROM_AFTER - 1)
                row = jnp.where(wanted >= FR, from_after[head, :, slot], row)
            next_ref[frame, :, columns] = row[0]
            other_ref[FR + frame, :, columns] = row[1]


def block_spec(array, blocks, base=0):
    shape = (1,) + array.shape[1:]
    zeros = (0,) * (len(shape) - 1)
    return pl.BlockSpec(shape, lambda i, *_: (base + jnp.minimum(i, blocks - 1),) + zeros)


class Task:
    def __init__(self, blocks, operands, in_specs, out_shape, out_specs, body):
        self.blocks, self.body = blocks, body
        self.operands, self.in_specs = operands, in_specs
        self.out_shape, self.out_specs = out_shape, out_specs


def attention_task(queries, sources, base):
    blocks = sources[0].shape[0]
    frames, tokens, head_size = queries[0].shape[1:]
    shape = like(blocks, NEAR, frames, tokens, head_size)
    return Task(
        blocks,
        [*queries, *sources],
        [block_spec(query, blocks, base) for query in queries]
        + [block_spec(source, blocks) for source in sources],
        [shape],
        [block_spec(shape, blocks)],
        attention_body,
    )


def blend_task(out, after, after_base, windows):
    blocks, halves, _, tokens, head_size = out.shape
    owned = FR // windows
    counts = [FR, owned + FROM_BEFORE] + [owned] * (windows - 3)
    shapes = [like(blocks, halves, count, tokens, head_size) for count in counts]
    return Task(
        blocks,
        [out, after],
        [block_spec(out, blocks), block_spec(after, blocks, after_base)],
        shapes,
        [block_spec(shape, blocks) for shape in shapes],
        functools.partial(blend_body, windows),
    )


def run_stage(tables, tasks, merged=True):
    steps = max(task.blocks for task in tasks)
    operands = [operand for task in tasks for operand in task.operands]
    shapes = [shape for task in tasks for shape in task.out_shape]
    windows = lax.axis_size("win")
    assert left_count(windows) == HOME_BASE
    _, halves, _, tokens, head_size = shapes[0].shape
    blocks = [task.blocks for task in tasks]
    lefts = [
        like(count, halves, HOME_BASE, tokens, head_size)
        for count in ([sum(blocks)] if merged else blocks)
    ]

    def kernel(*refs):
        table_refs, refs = refs[: len(tables)], refs[len(tables) :]
        in_refs, refs = refs[: len(operands)], refs[len(operands) :]
        out_refs, left_refs = refs[: len(shapes)], refs[len(shapes) :]
        step = pl.program_id(0)
        for index, task in enumerate(tasks):
            task_in, in_refs = in_refs[: len(task.operands)], in_refs[len(task.operands) :]
            task_out, out_refs = out_refs[: len(task.out_shape)], out_refs[len(task.out_shape) :]
            body = functools.partial(
                task.body,
                table_refs,
                task_in,
                task_out,
                left_refs[0 if merged else index],
                sum(blocks[:index]) if merged else 0,
            )
            if task.blocks == steps:
                body()
            else:
                pl.when(step < task.blocks)(body)

    outputs = pl.pallas_call(
        kernel,
        grid=(steps,),
        in_specs=[SMEM for _ in tables] + [spec for task in tasks for spec in task.in_specs],
        out_specs=[spec for task in tasks for spec in task.out_specs]
        + [pl.BlockSpec(left.shape, lambda i: (0,) * 5) for left in lefts],
        out_shape=shapes + lefts,
        compiler_params=params(),
        cost_estimate=NO_COST,
        name="stage",
    )(*tables, *operands)
    results = []
    for task in tasks:
        results.append(outputs[: len(task.out_shape)])
        outputs = outputs[len(task.out_shape) :]
    return results, outputs


def result_columns(half, base, width):
    head_size = width[1]
    column = (half * (HEADS // NEAR) + base) * head_size
    return pl.ds(pl.multiple_of(column, head_size), width[0] * head_size)


def place(tables, home, received, base, features, windows, targets):
    heads, halves, _, tokens, head_size = home.shape
    operands = [home, *received]

    def first_heads(operand):
        return pl.BlockSpec((heads,) + operand.shape[1:], lambda i: (0,) * len(operand.shape))

    def kernel(*refs):
        table_refs, refs = refs[: len(tables)], refs[len(tables) :]
        in_refs, refs = refs[: len(operands)], refs[len(operands) + len(targets) :]
        owned_ref, next_ref, other_ref, owned_rows, next_rows, sems = refs
        place_body(windows, table_refs, in_refs, (owned_rows, next_rows, other_ref))
        columns = result_columns(table_refs[-1][0], base, (heads, head_size))
        copies = [
            pltpu.make_async_copy(owned_rows, owned_ref.at[:, :, columns], sems.at[0]),
            pltpu.make_async_copy(next_rows, next_ref.at[:, :, columns], sems.at[1]),
        ]
        for copy in copies:
            copy.start()
        for copy in copies:
            copy.wait()

    other = like(FR + WF, tokens, heads * head_size)
    anywhere = pl.BlockSpec(memory_space=pl.ANY)
    *targets, other = pl.pallas_call(
        kernel,
        grid=(1,),
        in_specs=[SMEM for _ in tables]
        + [first_heads(operand) for operand in operands]
        + [anywhere for _ in targets],
        out_specs=[anywhere, anywhere, pl.BlockSpec(other.shape, lambda i: (0, 0, 0))],
        out_shape=[like(FR, tokens, features), like(WF, tokens, features), other],
        scratch_shapes=[
            pltpu.VMEM((FR, tokens, heads * head_size), jnp.bfloat16),
            pltpu.VMEM((WF, tokens, heads * head_size), jnp.bfloat16),
            pltpu.SemaphoreType.DMA((2,)),
        ],
        input_output_aliases={len(tables) + len(operands) + i: i for i in range(len(targets))},
        compiler_params=params(),
        cost_estimate=FILLER,
        name="place",
    )(*tables, *operands, *targets)
    return targets, other


def finish(near, others, bases, head_size, targets):
    def kernel(near_ref, *refs):
        in_refs, (owned_ref, next_ref, sems) = refs[: len(others)], refs[len(others) + 2 :]
        copies = []
        for index, (other_ref, base) in enumerate(zip(in_refs, bases)):
            heads = other_ref.shape[-1] // head_size
            columns = result_columns(NEAR - 1 - near_ref[0], base, (heads, head_size))
            copies += [
                pltpu.make_async_copy(
                    other_ref.at[pl.ds(0, FR)], owned_ref.at[:, :, columns], sems.at[2 * index]
                ),
                pltpu.make_async_copy(
                    other_ref.at[pl.ds(FR, WF)], next_ref.at[:, :, columns], sems.at[2 * index + 1]
                ),
            ]
        for copy in copies:
            copy.start()
        for copy in copies:
            copy.wait()

    anywhere = pl.BlockSpec(memory_space=pl.ANY)
    return pl.pallas_call(
        kernel,
        grid=(1,),
        in_specs=[SMEM]
        + [pl.BlockSpec(other.shape, lambda i: (0, 0, 0)) for other in others]
        + [anywhere for _ in targets],
        out_specs=[anywhere, anywhere],
        out_shape=[like(*target.shape) for target in targets],
        scratch_shapes=[pltpu.SemaphoreType.DMA((2 * len(others),))],
        input_output_aliases={1 + len(others) + i: i for i in range(2)},
        compiler_params=params(),
        cost_estimate=FILLER,
        name="finish",
    )(near, *others, *targets)


def exchange(array, bit):
    return lax.ppermute(array, "uly", [(i, i ^ bit) for i in range(lax.axis_size("uly"))])


def shift(array, step):
    count = lax.axis_size("win")
    return lax.ppermute(array, "win", [(i, (i + step) % count) for i in range(count)])


def after(array, *others):
    return lax.optimization_barrier((array, *others))[0] if others else array


def normalize(row_block, gain_vector):
    floats = row_block.astype(jnp.float32)
    mean_square = jnp.mean(floats * floats, axis=-1, keepdims=True)
    return (floats * lax.rsqrt(mean_square + 1e-06) * gain_vector).astype(jnp.bfloat16)


def head_attention(operands):
    query_head, key_head, value_head = operands
    scores = jnp.dot(query_head, key_head.T, preferred_element_type=jnp.float32) * (
        1.0 / math.sqrt(query_head.shape[-1])
    )
    row_max = jnp.max(scores, axis=-1, keepdims=True)
    exponent = jnp.exp(scores - row_max)
    weights = (exponent / jnp.sum(exponent, axis=-1, keepdims=True)).astype(jnp.bfloat16)
    return jnp.dot(weights, value_head, preferred_element_type=jnp.float32).astype(jnp.bfloat16)


def attend(operands):
    query_part, key_part, value_part = operands
    heads_here = query_part.shape[3]
    head_size = query_part.shape[4]
    token_count = query_part.shape[0] * query_part.shape[1]

    def flatten(tensor):
        return jnp.moveaxis(tensor.reshape(token_count, heads_here, head_size), 1, 0)

    result = lax.map(head_attention, (flatten(query_part), flatten(key_part), flatten(value_part)))
    return jnp.moveaxis(result, 0, 1).reshape(query_part.shape)


def table_lookup(table_row, wanted, length):
    entries = jnp.arange(length, dtype=jnp.int32)
    return jnp.sum(jnp.where(wanted[..., None] == entries, table_row, 0), axis=-1)


def send_owners(frame_rows, inverse, my_start, windows, capacity):
    slot_index = jnp.arange(capacity, dtype=jnp.int32)
    position_in = (inverse[:, None] - my_start) % windows + slot_index[None, :] * windows
    is_valid = (position_in < WF).reshape(-1)
    picked = jnp.take(frame_rows, jnp.minimum(position_in, WF - 1).reshape(-1), axis=0)
    picked = jnp.where(is_valid[:, None, None], picked, jnp.zeros_like(picked))
    packed = picked.reshape(windows, capacity, frame_rows.shape[1], frame_rows.shape[2])
    return lax.all_to_all(packed, "win", split_axis=0, concat_axis=0, tiled=True)


def combine_owned(received, window_start, blend_weight, my_phase, windows, frames_total, capacity):
    slot_index = jnp.arange(capacity, dtype=jnp.int32)
    source_pos = (my_phase - window_start[:, None]) % windows + slot_index[None, :] * windows
    arrived = source_pos < WF
    slot_at = (window_start[:, None] + source_pos) % frames_total // windows
    factor = table_lookup(blend_weight[:, None, :], source_pos, WF)
    owned_range = jnp.arange(FR, dtype=jnp.int32)
    mixing = jnp.where(
        (slot_at[None] == owned_range[:, None, None]) & arrived[None], factor[None], 0
    )
    mixing = mixing.reshape(FR, windows * capacity).astype(jnp.float32)
    numerator = jnp.dot(
        mixing.astype(jnp.bfloat16),
        received.reshape(windows * capacity, -1),
        preferred_element_type=jnp.float32,
    )
    denominator = jnp.sum(mixing, axis=1)
    owned = (numerator / denominator[:, None]).astype(jnp.bfloat16)
    return owned.reshape(FR, received.shape[2], received.shape[3])


def general(
    query_rows,
    key_rows,
    value_rows,
    query_gain,
    key_gain,
    window_start,
    owner_of_phase,
    blend_weight,
):
    windows = lax.axis_size("win")
    ulysses = lax.axis_size("uly")
    position = lax.axis_index("win")
    frames_total = FR * windows
    capacity = (WF + windows - 1) // windows
    shift_frames = FR // 2
    local_tokens = query_rows.shape[2]
    feature_count = query_rows.shape[3]
    groups = HEADS // ulysses
    head_size = feature_count // HEADS
    split_shape = (WF, local_tokens, ulysses, groups, head_size)
    query_heads = normalize(query_rows[0], query_gain).reshape(split_shape)
    key_heads = normalize(key_rows[0], key_gain).reshape(split_shape)
    value_heads = value_rows[0].reshape(split_shape)
    attended = attend(
        (
            lax.all_to_all(query_heads, "uly", split_axis=2, concat_axis=1, tiled=True),
            lax.all_to_all(key_heads, "uly", split_axis=2, concat_axis=1, tiled=True),
            lax.all_to_all(value_heads, "uly", split_axis=2, concat_axis=1, tiled=True),
        )
    )
    own_out = lax.all_to_all(attended, "uly", split_axis=1, concat_axis=2, tiled=True).reshape(
        WF, local_tokens, feature_count
    )
    phases = jnp.arange(windows, dtype=jnp.int32)
    inverse = jnp.sum(
        jnp.where(owner_of_phase[None, :] == phases[:, None], phases[None, :], 0), axis=1
    )
    my_start = window_start[position]
    my_phase = inverse[position]
    frame_range = jnp.arange(WF, dtype=jnp.int32)
    received = send_owners(own_out, inverse, my_start, windows, capacity)
    owned = combine_owned(
        received, window_start, blend_weight, my_phase, windows, frames_total, capacity
    )
    slot_index = jnp.arange(capacity, dtype=jnp.int32)
    target_pos = (my_phase - window_start[:, None] - shift_frames) % windows + slot_index[
        None, :
    ] * windows
    target_valid = (target_pos < WF).reshape(-1)
    target_slot = (
        (window_start[:, None] + shift_frames + target_pos) % frames_total // windows
    ).reshape(-1)
    outgoing = jnp.take(owned, target_slot, axis=0)
    outgoing = jnp.where(target_valid[:, None, None], outgoing, jnp.zeros_like(outgoing))
    outgoing = outgoing.reshape(windows, capacity, local_tokens, feature_count)
    returned = lax.all_to_all(outgoing, "win", split_axis=0, concat_axis=0, tiled=True)
    needed_phase = (my_start + shift_frames + frame_range) % windows
    source_owner = table_lookup(owner_of_phase[None, :], needed_phase, windows)
    flat_index = source_owner * capacity + frame_range // windows
    next_rows = jnp.take(
        returned.reshape(windows * capacity, local_tokens, feature_count), flat_index, axis=0
    )
    return (owned, next_rows[None])


def far_blocks(own):
    blocks = [own]
    bit = lax.axis_size("uly") // 2
    while bit >= NEAR:
        blocks += [exchange(block, bit) for block in blocks]
        bit //= 2
    return blocks


def pipelined(
    query_rows,
    key_rows,
    value_rows,
    query_gain,
    key_gain,
    window_start,
    owner_of_phase,
    blend_weight,
):
    windows = lax.axis_size("win")
    features = query_rows.shape[-1]
    head_size = features // HEADS
    near = lax.rem(lax.axis_index("uly"), NEAR).astype(jnp.int32).reshape(1)
    position = lax.axis_index("win").astype(jnp.int32).reshape(1)
    tables = (position, window_start, owner_of_phase, blend_weight, near)
    query_gain = query_gain.reshape(1, 1, features)
    key_gain = key_gain.reshape(1, 1, features)
    count = len(CHUNKS)
    bases = [sum(CHUNKS[:i]) for i in range(count)]

    groups = [CHUNKS[:1], CHUNKS[1:2], CHUNKS[2:]]
    own, *sent = split_heads(
        near, key_rows[0], key_gain, [sum(group) for group in groups], (value_rows[0],)
    )
    chunks = []
    queries = None
    for array, group in zip(sent, groups):
        other = exchange(after(array, *chunks[-1:]), 1)
        base = bases[len(chunks)]
        chunks += join_halves(own, base, other, group)
        if queries is None:
            own_queries, sent_queries = split_heads(
                near, after(query_rows[0], *chunks), query_gain, [sum(CHUNKS)]
            )
            queries = [own_queries, exchange(sent_queries, 1)]
    sources = [far_blocks(chunk) for chunk in chunks]

    attended, homes, received, others, heads = {}, {}, {}, {}, {}
    targets = ()

    def place_chunk(chunk, *earlier):
        return place(
            tables,
            after(homes[chunk], *earlier),
            received[chunk],
            bases[chunk],
            features,
            windows,
            targets,
        )

    for chunk in range(count + 1):
        tasks = []
        if chunk >= 1:
            tasks.append(blend_task(attended[chunk - 1], *heads[chunk - 1], windows))
        if chunk < count:
            tasks.append(attention_task(queries, sources[chunk], bases[chunk]))
        merged = chunk < count - 1 or len(tasks) == 1
        results, lefts = run_stage(tables, tasks, merged)
        gate = received[chunk - 2] if chunk >= 2 else ()
        lefts = [shift(after(left, *gate), -1) for left in reversed(lefts)]
        if chunk >= 1:
            homes[chunk - 1], *sent = results.pop(0)
            received[chunk - 1] = [
                shift(array, distance) for distance, array in enumerate(sent, 1)
            ] + lefts[-1:]
        if chunk < count:
            ((attended[chunk],),) = results
        if chunk >= 2:
            targets, others[chunk - 2] = place_chunk(
                chunk - 2, attended[chunk] if chunk < count else homes[chunk - 1]
            )
        if chunk < count:
            left = lefts[0]
            if 2 <= chunk:
                left = after(left, targets[0])
            heads[chunk] = (left, CHUNKS[chunk - 1] if merged and chunk >= 1 else 0)
    early = range(count - 2)
    arrived = [exchange(after(others[i], homes[count - 1]), 1) for i in early]
    targets = finish(near, arrived, [bases[i] for i in early], head_size, targets)
    targets, others[count - 1] = place_chunk(count - 1)
    late = range(count - 2, count)
    arrived = [exchange(others[i], 1) for i in late]
    owned, next_rows = finish(near, arrived, [bases[i] for i in late], head_size, targets)
    return (owned, next_rows[None])


def per_device(*operands):
    windows, ulysses = lax.axis_size("win"), lax.axis_size("uly")
    fits = windows >= 3 and FR % windows == 0 and left_count(windows) == HOME_BASE
    if fits and ulysses >= NEAR and ulysses & (ulysses - 1) == 0:
        return pipelined(*operands)
    return general(*operands)


def solution(mesh):
    placed = (
        P(("grp", "win"), None, "uly", None),
        P(("grp", "win"), None, "uly", None),
        P(("grp", "win"), None, "uly", None),
        P(),
        P(),
        P("grp"),
        P("grp"),
        P("grp", None),
    )
    return jax.shard_map(
        per_device,
        mesh=mesh,
        in_specs=placed,
        out_specs=(P(("grp", "win"), "uly", None), P(("grp", "win"), None, "uly", None)),
        check_vma=False,
    )
```

```python
import functools
import math

import jax
import jax.numpy as jnp
from jax import lax
from jax.experimental import pallas as pl
from jax.experimental.pallas import tpu as pltpu
from jax.sharding import PartitionSpec as P

HEADS = 40
WF = 16
FR = 12
MARGIN = WF - FR
SHIFT = FR // 2
HOME_BASE = 2 * MARGIN
FROM_BEFORE = HOME_BASE - SHIFT
FROM_AFTER = SHIFT + WF + MARGIN - HOME_BASE - FR
NEAR = 2
CHUNKS = (2, 4, 4, 4, 4, 2)
STEP_HEADS = 2
VMEM_LIMIT = 64 * 1024 * 1024


def params():
    return pltpu.CompilerParams(vmem_limit_bytes=VMEM_LIMIT)


def like(*shape):
    return jax.ShapeDtypeStruct(shape, jnp.bfloat16)


def cost(microseconds):
    return pl.CostEstimate(
        flops=int(microseconds * 1.15e9), bytes_accessed=0, transcendentals=0
    )


NORM_COST = 8.7
JOIN_COST = 8.7
REST_COST = 0.0
STAGE_COST = 0.0
BLEND_COST = 0.0
SWAP = 1
PLACE_COST = 6.0
TAIL_COST = 0.0
LATE_CHUNKS = 1
FREE = 2
SMEM = pl.BlockSpec(memory_space=pltpu.SMEM)


def split_heads(near, rows, gain, counts, plain=(), frames_per_step=8):
    frames, tokens, features = rows.shape
    head_size = features // HEADS
    kinds = (2,) * len(plain)
    heads = HEADS // NEAR

    def kernel(near_ref, rows_ref, gain_ref, *refs):
        plain_refs, out_refs = refs[: len(plain)], refs[len(plain) :]
        here = near_ref[0]
        squares = jnp.zeros((frames_per_step, tokens, head_size), jnp.float32)
        for head in range(HEADS):
            floats = rows_ref[:, :, head * head_size : (head + 1) * head_size].astype(jnp.float32)
            squares += floats * floats
        mean_square = jnp.sum(squares, axis=-1, keepdims=True) / features
        scale = jnp.broadcast_to(lax.rsqrt(mean_square + 1e-06), squares.shape)

        def put(out_ref, slot, half, head):
            column = pl.multiple_of((half * heads + head) * head_size, head_size)
            columns = pl.ds(column, head_size)
            floats = rows_ref[:, :, columns].astype(jnp.float32)
            normalized = (floats * scale * gain_ref[:, :, columns]).astype(jnp.bfloat16)
            if plain:
                out_ref[slot, 0] = normalized
                out_ref[slot, 1] = plain_refs[0][:, :, columns]
            else:
                out_ref[slot] = normalized

        for head in range(heads):
            put(out_refs[0], head, here, head)
        head = 0
        for out_ref in out_refs[1:]:
            for slot in range(out_ref.shape[0]):
                put(out_ref, slot, NEAR - 1 - here, head)
                head += 1

    block = pl.BlockSpec((frames_per_step, tokens, features), lambda i: (i, 0, 0))

    def out_spec(count):
        zeros = (0,) * (1 + len(kinds))
        return pl.BlockSpec(
            (count, *kinds, frames_per_step, tokens, head_size), lambda i: (*zeros, i, 0, 0)
        )

    return pl.pallas_call(
        kernel,
        grid=(frames // frames_per_step,),
        in_specs=[SMEM, block, pl.BlockSpec((1, 1, features), lambda i: (0, 0, 0))]
        + [block for _ in plain],
        out_specs=[out_spec(count) for count in (sum(counts), *counts)],
        out_shape=[
            like(count, *kinds, frames, tokens, head_size) for count in (sum(counts), *counts)
        ],
        compiler_params=params(),
        cost_estimate=cost(NORM_COST),
        name="norm_split",
    )(near, rows, gain, *plain)


def join_halves(own, base, other, counts):
    _, kinds, frames, tokens, head_size = own.shape
    bases = [sum(counts[:i]) for i in range(len(counts))]

    def out_spec(first, count):
        return pl.BlockSpec(
            (STEP_HEADS, kinds, NEAR, frames, tokens, head_size),
            lambda i: (jnp.clip(i - first // STEP_HEADS, 0, count // STEP_HEADS - 1),) + (0,) * 5,
        )

    def kernel(own_ref, other_ref, *out_refs):
        step = pl.program_id(0) * STEP_HEADS
        for out_ref, first, count in zip(out_refs, bases, counts):

            @pl.when((step >= first) & (step < first + count))
            def _():
                out_ref[:, :, 0] = own_ref[...]
                out_ref[:, :, 1] = other_ref[...]

    block = (STEP_HEADS, kinds, frames, tokens, head_size)
    return pl.pallas_call(
        kernel,
        grid=(sum(counts) // STEP_HEADS,),
        in_specs=[
            pl.BlockSpec(block, lambda i: (base // STEP_HEADS + i, 0, 0, 0, 0)),
            pl.BlockSpec(block, lambda i: (i, 0, 0, 0, 0)),
        ],
        out_specs=[out_spec(first, count) for first, count in zip(bases, counts)],
        out_shape=[
            like(count, kinds, NEAR, frames, tokens, head_size) for count in counts
        ],
        compiler_params=params(),
        cost_estimate=cost(JOIN_COST if len(counts) == 1 else REST_COST),
        name="join_halves",
    )(own, other)


def attention_body(tables, in_refs, out_refs, left_ref, left_base):
    query_refs, sources = in_refs[:NEAR], in_refs[NEAR:]
    (out_ref,) = out_refs
    _, frames, tokens, head_size = query_refs[0].shape
    rows = frames * tokens
    factor = math.log2(math.e) / math.sqrt(head_size)
    contract = (((1,), (1,)), ((), ()))
    left_slot = left_base + pl.program_id(0) * STEP_HEADS

    def scores_of(head, half):
        query = query_refs[half][head].reshape(rows, head_size)
        return [
            lax.dot_general(
                query,
                source[head, 0].reshape(NEAR * rows, head_size),
                contract,
                preferred_element_type=jnp.float32,
            )
            for source in sources
        ]

    pieces = [(head, half) for head in range(STEP_HEADS) for half in range(NEAR)]
    following = scores_of(*pieces[0])
    for index, (head, half) in enumerate(pieces):
        scores = following
        if index + 1 < len(pieces):
            following = scores_of(*pieces[index + 1])
        row_max = functools.reduce(jnp.maximum, scores)
        row_max = jnp.max(row_max, axis=-1, keepdims=True)
        exponents = [jnp.exp2((score - row_max) * factor) for score in scores]
        total = jnp.sum(functools.reduce(jnp.add, exponents), axis=-1, keepdims=True)
        inverse = 1.0 / total
        result = jnp.zeros((rows, head_size), jnp.float32)
        for exponent, source in zip(exponents, sources):
            weights = (exponent * inverse).astype(jnp.bfloat16)
            result += jnp.dot(
                weights,
                source[head, 1].reshape(NEAR * rows, head_size),
                preferred_element_type=jnp.float32,
            )
        result = result.astype(jnp.bfloat16).reshape(frames, tokens, head_size)
        out_ref[head, half] = result
        left_ref[left_slot + head, half] = result[:HOME_BASE]


def phase_of(owner_ref, wanted, windows):
    phase = jnp.int32(0)
    for index in range(windows):
        phase = jnp.where(owner_ref[index] == wanted, index, phase)
    return phase


def first_owned(phase, windows):
    return lax.rem(phase + (windows - 1) * HOME_BASE, windows)


def extra_owned(windows):
    return [i for i in range(FR // windows) if windows * (i + 1) > FROM_AFTER]


def left_count(windows):
    return FROM_AFTER + len(extra_owned(windows))


def blend_body(windows, tables, in_refs, out_refs, left_ref, left_base):
    place_ref, start_ref, owner_ref, weight_ref, _ = tables
    out_ref, after_ref = in_refs
    home_ref, *sent_refs = out_refs
    here = place_ref[0]
    after = lax.rem(here + 1, windows)
    offset = start_ref[here] - here * FR
    offset_after = start_ref[after] - after * FR
    left_slots = pl.ds(left_base + pl.program_id(0) * STEP_HEADS, STEP_HEADS)
    for frame in range(FR):
        place = frame + HOME_BASE - offset
        if frame + HOME_BASE < WF:
            weight = weight_ref[here, place].astype(jnp.float32)
        else:
            valid = place < WF
            place = jnp.minimum(place, WF - 1)
            weight = jnp.where(valid, weight_ref[here, place], 0).astype(jnp.float32)
        numerator = out_ref[:, :, place].astype(jnp.float32) * weight
        denominator = weight
        if frame + HOME_BASE >= FR:
            slot = frame + HOME_BASE - FR - offset_after
            valid = slot >= 0
            slot = jnp.maximum(slot, 0)
            weight = jnp.where(valid, weight_ref[after, slot], 0).astype(jnp.float32)
            numerator += after_ref[:, :, slot].astype(jnp.float32) * weight
            denominator += weight
        home_ref[:, :, frame] = (numerator / denominator).astype(jnp.bfloat16)
    for distance in range(1, windows):
        target = lax.rem(here + distance, windows)
        first = first_owned(phase_of(owner_ref, target, windows), windows)
        if distance == windows - 1:
            left_ref[left_slots, :, :FROM_AFTER] = home_ref[:, :, :FROM_AFTER]
            for slot, index in enumerate(extra_owned(windows)):
                left_ref[left_slots, :, FROM_AFTER + slot] = home_ref[:, :, first + index * windows]
            continue
        sent_ref = sent_refs[distance - 1]
        for index in range(FR // windows):
            sent_ref[:, :, index] = home_ref[:, :, first + index * windows]
        if distance == 1:
            sent_ref[:, :, FR // windows :] = home_ref[:, :, FR - FROM_BEFORE :]


def place_body(windows, tables, in_refs, out_refs):
    place_ref, start_ref, owner_ref = tables[:3]
    home_ref, *received = in_refs
    owned_ref, next_ref, other_ref = out_refs
    here = place_ref[0]
    first = first_owned(phase_of(owner_ref, here, windows), windows)
    slot_base = (first + HOME_BASE) // windows
    count = FR // windows
    extra = extra_owned(windows)
    heads, _, _, _, head_size = home_ref.shape
    offset = start_ref[here] - here * FR + SHIFT - HOME_BASE
    from_before, from_after = received[0], received[-1]
    for head in range(heads):
        columns = slice(head * head_size, (head + 1) * head_size)
        for distance in range(windows):
            source = lax.rem(here + windows - distance, windows)
            for index in range(count):
                slot = lax.rem(source * count + slot_base + index, FR)
                if distance == 0:
                    row = home_ref[head, :, first + index * windows]
                elif distance < windows - 1:
                    row = received[distance - 1][head, :, index]
                elif index in extra:
                    row = received[distance - 1][head, :, FROM_AFTER + extra.index(index)]
                else:
                    row = received[distance - 1][head, :, first + index * windows]
                owned_ref[slot, :, columns] = row[0]
                other_ref[slot, :, columns] = row[1]
        for frame in range(WF):
            wanted = offset + frame
            row = home_ref[head, :, jnp.clip(wanted, 0, FR - 1)]
            if frame < FROM_BEFORE:
                slot = jnp.clip(wanted + FROM_BEFORE, 0, FROM_BEFORE - 1)
                row = jnp.where(wanted < 0, from_before[head, :, count + slot], row)
            if frame + MARGIN + SHIFT - HOME_BASE >= FR:
                slot = jnp.clip(wanted - FR, 0, FROM_AFTER - 1)
                row = jnp.where(wanted >= FR, from_after[head, :, slot], row)
            next_ref[frame, :, columns] = row[0]
            other_ref[FR + frame, :, columns] = row[1]


def block_spec(array, blocks, base=0):
    shape = (STEP_HEADS,) + array.shape[1:]
    zeros = (0,) * (len(shape) - 1)
    return pl.BlockSpec(
        shape, lambda i: (base // STEP_HEADS + jnp.minimum(i, blocks - 1),) + zeros
    )


class Task:
    def __init__(self, blocks, operands, in_specs, out_shape, out_specs, body):
        self.blocks, self.body = blocks, body
        self.operands, self.in_specs = operands, in_specs
        self.out_shape, self.out_specs = out_shape, out_specs


def attention_task(queries, sources):
    heads = sources[0].shape[0]
    blocks = heads // STEP_HEADS
    frames, tokens, head_size = queries[0][0].shape[1:]
    shape = like(heads, NEAR, frames, tokens, head_size)
    return Task(
        blocks,
        [query for query, _ in queries] + sources,
        [block_spec(query, blocks, base) for query, base in queries]
        + [block_spec(source, blocks) for source in sources],
        [shape],
        [block_spec(shape, blocks)],
        attention_body,
    )


def blend_task(out, after, after_base, windows):
    heads, halves, _, tokens, head_size = out.shape
    blocks = heads // STEP_HEADS
    owned = FR // windows
    counts = [FR, owned + FROM_BEFORE] + [owned] * (windows - 3)
    shapes = [like(heads, halves, count, tokens, head_size) for count in counts]
    return Task(
        blocks,
        [out, after],
        [block_spec(out, blocks), block_spec(after, blocks, after_base)],
        shapes,
        [block_spec(shape, blocks) for shape in shapes],
        functools.partial(blend_body, windows),
    )


def run_stage(tables, tasks, weight, merged=True):
    steps = max(task.blocks for task in tasks)
    operands = [operand for task in tasks for operand in task.operands]
    shapes = [shape for task in tasks for shape in task.out_shape]
    windows = lax.axis_size("win")
    assert left_count(windows) == HOME_BASE
    _, halves, _, tokens, head_size = shapes[0].shape
    blocks = [task.blocks * STEP_HEADS for task in tasks]
    lefts = [
        like(count, halves, HOME_BASE, tokens, head_size)
        for count in ([sum(blocks)] if merged else blocks)
    ]

    def kernel(*refs):
        table_refs, refs = refs[: len(tables)], refs[len(tables) :]
        in_refs, refs = refs[: len(operands)], refs[len(operands) :]
        out_refs, left_refs = refs[: len(shapes)], refs[len(shapes) :]
        step = pl.program_id(0)
        for index, task in enumerate(tasks):
            task_in, in_refs = in_refs[: len(task.operands)], in_refs[len(task.operands) :]
            task_out, out_refs = out_refs[: len(task.out_shape)], out_refs[len(task.out_shape) :]
            body = functools.partial(
                task.body,
                table_refs,
                task_in,
                task_out,
                left_refs[0 if merged else index],
                sum(blocks[:index]) if merged else 0,
            )
            if task.blocks == steps:
                body()
            else:
                pl.when(step < task.blocks)(body)

    outputs = pl.pallas_call(
        kernel,
        grid=(steps,),
        in_specs=[SMEM for _ in tables] + [spec for task in tasks for spec in task.in_specs],
        out_specs=[spec for task in tasks for spec in task.out_specs]
        + [pl.BlockSpec(left.shape, lambda i: (0,) * 5) for left in lefts],
        out_shape=shapes + lefts,
        compiler_params=params(),
        cost_estimate=cost(weight),
        name="stage",
    )(*tables, *operands)
    results = []
    for task in tasks:
        results.append(outputs[: len(task.out_shape)])
        outputs = outputs[len(task.out_shape) :]
    return results, outputs


def result_columns(half, base, width):
    head_size = width[1]
    column = (half * (HEADS // NEAR) + base) * head_size
    return pl.ds(pl.multiple_of(column, head_size), width[0] * head_size)


def place(tables, home, received, base, features, windows, targets, other, other_base, other_heads, weight):
    heads, halves, _, tokens, head_size = home.shape
    operands = [home, *received]
    earlier = [*targets, *([] if other is None else [other])]
    slots = ([0, 1] if targets else []) + ([] if other is None else [2])

    def first_heads(operand):
        return pl.BlockSpec((heads,) + operand.shape[1:], lambda i: (0,) * len(operand.shape))

    def kernel(*refs):
        table_refs, refs = refs[: len(tables)], refs[len(tables) :]
        in_refs, refs = refs[: len(operands)], refs[len(operands) + len(earlier) :]
        owned_ref, next_ref, other_ref, owned_rows, next_rows, other_rows, sems = refs
        place_body(windows, table_refs, in_refs, (owned_rows, next_rows, other_rows))
        columns = result_columns(table_refs[-1][0], base, (heads, head_size))
        other_columns = pl.ds(other_base * head_size, heads * head_size)
        copies = [
            pltpu.make_async_copy(other_rows, other_ref.at[:, :, other_columns], sems.at[2]),
            pltpu.make_async_copy(owned_rows, owned_ref.at[:, :, columns], sems.at[0]),
            pltpu.make_async_copy(next_rows, next_ref.at[:, :, columns], sems.at[1]),
        ]
        for copy in copies:
            copy.start()
        for copy in copies:
            copy.wait()

    anywhere = pl.BlockSpec(memory_space=pl.ANY)
    *targets, other = pl.pallas_call(
        kernel,
        grid=(1,),
        in_specs=[SMEM for _ in tables]
        + [first_heads(operand) for operand in operands]
        + [anywhere for _ in earlier],
        out_specs=[anywhere] * 3,
        out_shape=[
            like(FR, tokens, features),
            like(WF, tokens, features),
            like(FR + WF, tokens, other_heads * head_size),
        ],
        scratch_shapes=[
            pltpu.VMEM((FR, tokens, heads * head_size), jnp.bfloat16),
            pltpu.VMEM((WF, tokens, heads * head_size), jnp.bfloat16),
            pltpu.VMEM((FR + WF, tokens, heads * head_size), jnp.bfloat16),
            pltpu.SemaphoreType.DMA((3,)),
        ],
        input_output_aliases={
            len(tables) + len(operands) + i: slot for i, slot in enumerate(slots)
        },
        compiler_params=params(),
        cost_estimate=cost(weight),
        name="place",
    )(*tables, *operands, *earlier)
    return targets, other


def finish(near, others, bases, head_size, targets):
    def kernel(near_ref, *refs):
        in_refs, (owned_ref, next_ref, sems) = refs[: len(others)], refs[len(others) + 2 :]
        copies = []
        for index, (other_ref, base) in enumerate(zip(in_refs, bases)):
            heads = other_ref.shape[-1] // head_size
            columns = result_columns(NEAR - 1 - near_ref[0], base, (heads, head_size))
            copies += [
                pltpu.make_async_copy(
                    other_ref.at[pl.ds(0, FR)], owned_ref.at[:, :, columns], sems.at[2 * index]
                ),
                pltpu.make_async_copy(
                    other_ref.at[pl.ds(FR, WF)], next_ref.at[:, :, columns], sems.at[2 * index + 1]
                ),
            ]
        for copy in copies:
            copy.start()
        for copy in copies:
            copy.wait()

    anywhere = pl.BlockSpec(memory_space=pl.ANY)
    return pl.pallas_call(
        kernel,
        grid=(1,),
        in_specs=[SMEM]
        + [pl.BlockSpec(other.shape, lambda i: (0, 0, 0)) for other in others]
        + [anywhere for _ in targets],
        out_specs=[anywhere, anywhere],
        out_shape=[like(*target.shape) for target in targets],
        scratch_shapes=[pltpu.SemaphoreType.DMA((2 * len(others),))],
        input_output_aliases={1 + len(others) + i: i for i in range(2)},
        compiler_params=params(),
        cost_estimate=cost(TAIL_COST),
        name="finish",
    )(near, *others, *targets)


def exchange(array, bit):
    return lax.ppermute(array, "uly", [(i, i ^ bit) for i in range(lax.axis_size("uly"))])


def shift(array, step):
    count = lax.axis_size("win")
    return lax.ppermute(array, "win", [(i, (i + step) % count) for i in range(count)])


def after(array, *others):
    return lax.optimization_barrier((array, *others))[0] if others else array


def normalize(row_block, gain_vector):
    floats = row_block.astype(jnp.float32)
    mean_square = jnp.mean(floats * floats, axis=-1, keepdims=True)
    return (floats * lax.rsqrt(mean_square + 1e-06) * gain_vector).astype(jnp.bfloat16)


def head_attention(operands):
    query_head, key_head, value_head = operands
    scores = jnp.dot(query_head, key_head.T, preferred_element_type=jnp.float32) * (
        1.0 / math.sqrt(query_head.shape[-1])
    )
    row_max = jnp.max(scores, axis=-1, keepdims=True)
    exponent = jnp.exp(scores - row_max)
    weights = (exponent / jnp.sum(exponent, axis=-1, keepdims=True)).astype(jnp.bfloat16)
    return jnp.dot(weights, value_head, preferred_element_type=jnp.float32).astype(jnp.bfloat16)


def attend(operands):
    query_part, key_part, value_part = operands
    heads_here = query_part.shape[3]
    head_size = query_part.shape[4]
    token_count = query_part.shape[0] * query_part.shape[1]

    def flatten(tensor):
        return jnp.moveaxis(tensor.reshape(token_count, heads_here, head_size), 1, 0)

    result = lax.map(head_attention, (flatten(query_part), flatten(key_part), flatten(value_part)))
    return jnp.moveaxis(result, 0, 1).reshape(query_part.shape)


def table_lookup(table_row, wanted, length):
    entries = jnp.arange(length, dtype=jnp.int32)
    return jnp.sum(jnp.where(wanted[..., None] == entries, table_row, 0), axis=-1)


def send_owners(frame_rows, inverse, my_start, windows, capacity):
    slot_index = jnp.arange(capacity, dtype=jnp.int32)
    position_in = (inverse[:, None] - my_start) % windows + slot_index[None, :] * windows
    is_valid = (position_in < WF).reshape(-1)
    picked = jnp.take(frame_rows, jnp.minimum(position_in, WF - 1).reshape(-1), axis=0)
    picked = jnp.where(is_valid[:, None, None], picked, jnp.zeros_like(picked))
    packed = picked.reshape(windows, capacity, frame_rows.shape[1], frame_rows.shape[2])
    return lax.all_to_all(packed, "win", split_axis=0, concat_axis=0, tiled=True)


def combine_owned(received, window_start, blend_weight, my_phase, windows, frames_total, capacity):
    slot_index = jnp.arange(capacity, dtype=jnp.int32)
    source_pos = (my_phase - window_start[:, None]) % windows + slot_index[None, :] * windows
    arrived = source_pos < WF
    slot_at = (window_start[:, None] + source_pos) % frames_total // windows
    factor = table_lookup(blend_weight[:, None, :], source_pos, WF)
    owned_range = jnp.arange(FR, dtype=jnp.int32)
    mixing = jnp.where(
        (slot_at[None] == owned_range[:, None, None]) & arrived[None], factor[None], 0
    )
    mixing = mixing.reshape(FR, windows * capacity).astype(jnp.float32)
    numerator = jnp.dot(
        mixing.astype(jnp.bfloat16),
        received.reshape(windows * capacity, -1),
        preferred_element_type=jnp.float32,
    )
    denominator = jnp.sum(mixing, axis=1)
    owned = (numerator / denominator[:, None]).astype(jnp.bfloat16)
    return owned.reshape(FR, received.shape[2], received.shape[3])


def general(
    query_rows,
    key_rows,
    value_rows,
    query_gain,
    key_gain,
    window_start,
    owner_of_phase,
    blend_weight,
):
    windows = lax.axis_size("win")
    ulysses = lax.axis_size("uly")
    position = lax.axis_index("win")
    frames_total = FR * windows
    capacity = (WF + windows - 1) // windows
    shift_frames = FR // 2
    local_tokens = query_rows.shape[2]
    feature_count = query_rows.shape[3]
    groups = HEADS // ulysses
    head_size = feature_count // HEADS
    split_shape = (WF, local_tokens, ulysses, groups, head_size)
    query_heads = normalize(query_rows[0], query_gain).reshape(split_shape)
    key_heads = normalize(key_rows[0], key_gain).reshape(split_shape)
    value_heads = value_rows[0].reshape(split_shape)
    attended = attend(
        (
            lax.all_to_all(query_heads, "uly", split_axis=2, concat_axis=1, tiled=True),
            lax.all_to_all(key_heads, "uly", split_axis=2, concat_axis=1, tiled=True),
            lax.all_to_all(value_heads, "uly", split_axis=2, concat_axis=1, tiled=True),
        )
    )
    own_out = lax.all_to_all(attended, "uly", split_axis=1, concat_axis=2, tiled=True).reshape(
        WF, local_tokens, feature_count
    )
    phases = jnp.arange(windows, dtype=jnp.int32)
    inverse = jnp.sum(
        jnp.where(owner_of_phase[None, :] == phases[:, None], phases[None, :], 0), axis=1
    )
    my_start = window_start[position]
    my_phase = inverse[position]
    frame_range = jnp.arange(WF, dtype=jnp.int32)
    received = send_owners(own_out, inverse, my_start, windows, capacity)
    owned = combine_owned(
        received, window_start, blend_weight, my_phase, windows, frames_total, capacity
    )
    slot_index = jnp.arange(capacity, dtype=jnp.int32)
    target_pos = (my_phase - window_start[:, None] - shift_frames) % windows + slot_index[
        None, :
    ] * windows
    target_valid = (target_pos < WF).reshape(-1)
    target_slot = (
        (window_start[:, None] + shift_frames + target_pos) % frames_total // windows
    ).reshape(-1)
    outgoing = jnp.take(owned, target_slot, axis=0)
    outgoing = jnp.where(target_valid[:, None, None], outgoing, jnp.zeros_like(outgoing))
    outgoing = outgoing.reshape(windows, capacity, local_tokens, feature_count)
    returned = lax.all_to_all(outgoing, "win", split_axis=0, concat_axis=0, tiled=True)
    needed_phase = (my_start + shift_frames + frame_range) % windows
    source_owner = table_lookup(owner_of_phase[None, :], needed_phase, windows)
    flat_index = source_owner * capacity + frame_range // windows
    next_rows = jnp.take(
        returned.reshape(windows * capacity, local_tokens, feature_count), flat_index, axis=0
    )
    return (owned, next_rows[None])


def far_blocks(own):
    blocks = [own]
    bit = lax.axis_size("uly") // 2
    while bit >= NEAR:
        blocks += [exchange(block, bit) for block in blocks]
        bit //= 2
    return blocks


def pipelined(
    query_rows,
    key_rows,
    value_rows,
    query_gain,
    key_gain,
    window_start,
    owner_of_phase,
    blend_weight,
):
    windows = lax.axis_size("win")
    features = query_rows.shape[-1]
    head_size = features // HEADS
    near = lax.rem(lax.axis_index("uly"), NEAR).astype(jnp.int32).reshape(1)
    position = lax.axis_index("win").astype(jnp.int32).reshape(1)
    tables = (position, window_start, owner_of_phase, blend_weight, near)
    query_gain = query_gain.reshape(1, 1, features)
    key_gain = key_gain.reshape(1, 1, features)
    count = len(CHUNKS)
    bases = [sum(CHUNKS[:i]) for i in range(count)]

    groups = [CHUNKS[:1], CHUNKS[1:2], CHUNKS[2:]]
    own, *sent = split_heads(
        near, key_rows[0], key_gain, [sum(group) for group in groups], (value_rows[0],)
    )
    chunks, sources = [], {}

    def join_group(index, *earlier):
        other = exchange(after(sent[index], *chunks[:1]), 1)
        chunks.extend(
            join_halves(own, bases[len(chunks)], after(other, *earlier), groups[index])
        )

    join_group(0)
    sources[0] = far_blocks(chunks[0])
    own_queries, *sent_queries = split_heads(
        near, after(query_rows[0], chunks[0]), query_gain, [CHUNKS[0], sum(CHUNKS[1:])]
    )
    first_queries, later_queries = [exchange(array, 1) for array in sent_queries]
    join_group(1, own_queries)
    sources[1] = far_blocks(chunks[1])

    attended, homes, received, others = {}, {}, {}, {}
    targets = ()

    def shift_around(arrays, *earlier):
        return [
            shift(after(array, *earlier), distance) for distance, array in enumerate(arrays, 1)
        ]

    early = count - LATE_CHUNKS
    early_heads = sum(CHUNKS[:early])

    def place_chunk(chunk, *earlier):
        late = chunk >= early
        targets_now, others[late] = place(
            tables,
            after(homes[chunk], *earlier),
            received[chunk],
            bases[chunk],
            features,
            windows,
            targets,
            others.get(late),
            bases[chunk] - early_heads if late else bases[chunk],
            sum(CHUNKS) - early_heads if late else early_heads,
            TAIL_COST if chunk >= count - FREE else PLACE_COST,
        )
        return targets_now

    arrived, waiting = {}, {}

    def attend(chunk, *earlier):
        queries = (after(own_queries, *earlier), bases[chunk]), (
            (later_queries, bases[chunk] - bases[1]) if chunk else (first_queries, 0)
        )
        (((attended[chunk],),), (left,)) = run_stage(
            tables, [attention_task(queries, sources[chunk])], STAGE_COST
        )
        return left

    def mix(chunk, *earlier):
        ready = after(arrived[chunk], *earlier)
        (((homes[chunk], *waiting[chunk]),), (left,)) = run_stage(
            tables, [blend_task(attended[chunk], ready, 0, windows)], BLEND_COST
        )
        received[chunk] = [shift(left, -1)]

    def send_around(chunk, *earlier):
        received[chunk] = [
            shift(after(array, *earlier), distance)
            for distance, array in enumerate(waiting[chunk], 1)
        ] + received[chunk]

    swapped = SWAP if count > 3 else 0
    for chunk in range(count - swapped):
        left = attend(chunk, homes[chunk - 1] if chunk else chunks[1])
        gate = received[chunk - 1] if chunk else []
        arrived[chunk] = shift(after(left, *gate), -1)
        if chunk >= 1:
            send_around(chunk - 1, attended[chunk])
        if chunk >= 2:
            targets = place_chunk(chunk - 2, attended[chunk])
        if chunk == count - 1 - swapped and swapped:
            break
        mix(chunk, *targets[:1])
        if chunk == 0:
            join_group(2, homes[0])
            for later in range(2, count):
                sources[later] = far_blocks(chunks[later])
    if swapped:
        left = attend(count - 1, attended[count - 2], targets[0])
        arrived[count - 1] = shift(left, -1)
        mix(count - 2, attended[count - 1])
        send_around(count - 2)
        targets = place_chunk(count - 3, homes[count - 2])
        mix(count - 1, homes[count - 2])
    send_around(count - 1)
    targets = place_chunk(count - 2, homes[count - 1])
    if LATE_CHUNKS > 1:
        arrived = exchange(after(others[False], homes[count - 1]), 1)
    else:
        arrived = exchange(others[False], 1)
    targets = finish(near, [arrived], [0], head_size, targets)
    targets = place_chunk(count - 1)
    owned, next_rows = finish(
        near, [exchange(others[True], 1)], [early_heads], head_size, targets
    )
    return (owned, next_rows[None])


def per_device(*operands):
    windows, ulysses = lax.axis_size("win"), lax.axis_size("uly")
    fits = windows >= 3 and FR % windows == 0 and left_count(windows) == HOME_BASE
    if fits and ulysses >= NEAR and ulysses & (ulysses - 1) == 0:
        return pipelined(*operands)
    return general(*operands)


def solution(mesh):
    placed = (
        P(("grp", "win"), None, "uly", None),
        P(("grp", "win"), None, "uly", None),
        P(("grp", "win"), None, "uly", None),
        P(),
        P(),
        P("grp"),
        P("grp"),
        P("grp", None),
    )
    return jax.shard_map(
        per_device,
        mesh=mesh,
        in_specs=placed,
        out_specs=(P(("grp", "win"), "uly", None), P(("grp", "win"), None, "uly", None)),
        check_vma=False,
    )
```

```python
import functools
import math

import jax
import jax.numpy as jnp
from jax import lax
from jax.experimental import pallas as pl
from jax.experimental.pallas import tpu as pltpu
from jax.sharding import PartitionSpec as P

HEADS = 40
WF = 16
FR = 12
MARGIN = WF - FR
SHIFT = FR // 2
HOME_BASE = 2 * MARGIN
FROM_BEFORE = HOME_BASE - SHIFT
FROM_AFTER = SHIFT + WF + MARGIN - HOME_BASE - FR
NEAR = 2
CHUNKS = (2, 4, 4, 4, 4, 2)
STEP_HEADS = 2
VMEM_LIMIT = 64 * 1024 * 1024


def params():
    return pltpu.CompilerParams(vmem_limit_bytes=VMEM_LIMIT)


def like(*shape):
    return jax.ShapeDtypeStruct(shape, jnp.bfloat16)


def cost(microseconds):
    return pl.CostEstimate(
        flops=int(microseconds * 1.15e9), bytes_accessed=0, transcendentals=0
    )


NORM_COST = 8.7
JOIN_COST = 8.7
REST_COST = 0.0
STAGE_COST = 0.0
BLEND_COST = 0.0
SWAP = 1
PLACE_COST = 7.5
TAIL_COST = 0.0
LATE_CHUNKS = 1
FREE = 1
P3_TIE = 0
CHAIN = 1
OX_TIE = 0
SMEM = pl.BlockSpec(memory_space=pltpu.SMEM)


def split_heads(near, rows, gain, counts, plain=(), frames_per_step=8):
    frames, tokens, features = rows.shape
    head_size = features // HEADS
    kinds = (2,) * len(plain)
    heads = HEADS // NEAR

    def kernel(near_ref, rows_ref, gain_ref, *refs):
        plain_refs, out_refs = refs[: len(plain)], refs[len(plain) :]
        here = near_ref[0]
        squares = jnp.zeros((frames_per_step, tokens, head_size), jnp.float32)
        for head in range(HEADS):
            floats = rows_ref[:, :, head * head_size : (head + 1) * head_size].astype(jnp.float32)
            squares += floats * floats
        mean_square = jnp.sum(squares, axis=-1, keepdims=True) / features
        scale = jnp.broadcast_to(lax.rsqrt(mean_square + 1e-06), squares.shape)

        def put(out_ref, slot, half, head):
            column = pl.multiple_of((half * heads + head) * head_size, head_size)
            columns = pl.ds(column, head_size)
            floats = rows_ref[:, :, columns].astype(jnp.float32)
            normalized = (floats * scale * gain_ref[:, :, columns]).astype(jnp.bfloat16)
            if plain:
                out_ref[slot, 0] = normalized
                out_ref[slot, 1] = plain_refs[0][:, :, columns]
            else:
                out_ref[slot] = normalized

        for head in range(heads):
            put(out_refs[0], head, here, head)
        head = 0
        for out_ref in out_refs[1:]:
            for slot in range(out_ref.shape[0]):
                put(out_ref, slot, NEAR - 1 - here, head)
                head += 1

    block = pl.BlockSpec((frames_per_step, tokens, features), lambda i: (i, 0, 0))

    def out_spec(count):
        zeros = (0,) * (1 + len(kinds))
        return pl.BlockSpec(
            (count, *kinds, frames_per_step, tokens, head_size), lambda i: (*zeros, i, 0, 0)
        )

    return pl.pallas_call(
        kernel,
        grid=(frames // frames_per_step,),
        in_specs=[SMEM, block, pl.BlockSpec((1, 1, features), lambda i: (0, 0, 0))]
        + [block for _ in plain],
        out_specs=[out_spec(count) for count in (sum(counts), *counts)],
        out_shape=[
            like(count, *kinds, frames, tokens, head_size) for count in (sum(counts), *counts)
        ],
        compiler_params=params(),
        cost_estimate=cost(NORM_COST),
        name="norm_split",
    )(near, rows, gain, *plain)


def join_halves(own, base, other, counts):
    _, kinds, frames, tokens, head_size = own.shape
    bases = [sum(counts[:i]) for i in range(len(counts))]

    def out_spec(first, count):
        return pl.BlockSpec(
            (STEP_HEADS, kinds, NEAR, frames, tokens, head_size),
            lambda i: (jnp.clip(i - first // STEP_HEADS, 0, count // STEP_HEADS - 1),) + (0,) * 5,
        )

    def kernel(own_ref, other_ref, *out_refs):
        step = pl.program_id(0) * STEP_HEADS
        for out_ref, first, count in zip(out_refs, bases, counts):

            @pl.when((step >= first) & (step < first + count))
            def _():
                out_ref[:, :, 0] = own_ref[...]
                out_ref[:, :, 1] = other_ref[...]

    block = (STEP_HEADS, kinds, frames, tokens, head_size)
    return pl.pallas_call(
        kernel,
        grid=(sum(counts) // STEP_HEADS,),
        in_specs=[
            pl.BlockSpec(block, lambda i: (base // STEP_HEADS + i, 0, 0, 0, 0)),
            pl.BlockSpec(block, lambda i: (i, 0, 0, 0, 0)),
        ],
        out_specs=[out_spec(first, count) for first, count in zip(bases, counts)],
        out_shape=[
            like(count, kinds, NEAR, frames, tokens, head_size) for count in counts
        ],
        compiler_params=params(),
        cost_estimate=cost(JOIN_COST if len(counts) == 1 else REST_COST),
        name="join_halves",
    )(own, other)


def attention_body(tables, in_refs, out_refs, left_ref, left_base):
    query_refs, sources = in_refs[:NEAR], in_refs[NEAR:]
    (out_ref,) = out_refs
    _, frames, tokens, head_size = query_refs[0].shape
    rows = frames * tokens
    factor = math.log2(math.e) / math.sqrt(head_size)
    contract = (((1,), (1,)), ((), ()))
    left_slot = left_base + pl.program_id(0) * STEP_HEADS

    def scores_of(head, half):
        query = query_refs[half][head].reshape(rows, head_size)
        return [
            lax.dot_general(
                query,
                source[head, 0].reshape(NEAR * rows, head_size),
                contract,
                preferred_element_type=jnp.float32,
            )
            for source in sources
        ]

    pieces = [(head, half) for head in range(STEP_HEADS) for half in range(NEAR)]
    following = scores_of(*pieces[0])
    for index, (head, half) in enumerate(pieces):
        scores = following
        if index + 1 < len(pieces):
            following = scores_of(*pieces[index + 1])
        row_max = functools.reduce(jnp.maximum, scores)
        row_max = jnp.max(row_max, axis=-1, keepdims=True)
        exponents = [jnp.exp2((score - row_max) * factor) for score in scores]
        total = jnp.sum(functools.reduce(jnp.add, exponents), axis=-1, keepdims=True)
        inverse = 1.0 / total
        result = jnp.zeros((rows, head_size), jnp.float32)
        for exponent, source in zip(exponents, sources):
            weights = (exponent * inverse).astype(jnp.bfloat16)
            result += jnp.dot(
                weights,
                source[head, 1].reshape(NEAR * rows, head_size),
                preferred_element_type=jnp.float32,
            )
        result = result.astype(jnp.bfloat16).reshape(frames, tokens, head_size)
        out_ref[head, half] = result
        left_ref[left_slot + head, half] = result[:HOME_BASE]


def phase_of(owner_ref, wanted, windows):
    phase = jnp.int32(0)
    for index in range(windows):
        phase = jnp.where(owner_ref[index] == wanted, index, phase)
    return phase


def first_owned(phase, windows):
    return lax.rem(phase + (windows - 1) * HOME_BASE, windows)


def extra_owned(windows):
    return [i for i in range(FR // windows) if windows * (i + 1) > FROM_AFTER]


def left_count(windows):
    return FROM_AFTER + len(extra_owned(windows))


def blend_body(windows, tables, in_refs, out_refs, left_ref, left_base):
    place_ref, start_ref, owner_ref, weight_ref, _ = tables
    out_ref, after_ref = in_refs
    home_ref, *sent_refs = out_refs
    here = place_ref[0]
    after = lax.rem(here + 1, windows)
    offset = start_ref[here] - here * FR
    offset_after = start_ref[after] - after * FR
    left_slots = pl.ds(left_base + pl.program_id(0) * STEP_HEADS, STEP_HEADS)
    for frame in range(FR):
        place = frame + HOME_BASE - offset
        if frame + HOME_BASE < WF:
            weight = weight_ref[here, place].astype(jnp.float32)
        else:
            valid = place < WF
            place = jnp.minimum(place, WF - 1)
            weight = jnp.where(valid, weight_ref[here, place], 0).astype(jnp.float32)
        numerator = out_ref[:, :, place].astype(jnp.float32) * weight
        denominator = weight
        if frame + HOME_BASE >= FR:
            slot = frame + HOME_BASE - FR - offset_after
            valid = slot >= 0
            slot = jnp.maximum(slot, 0)
            weight = jnp.where(valid, weight_ref[after, slot], 0).astype(jnp.float32)
            numerator += after_ref[:, :, slot].astype(jnp.float32) * weight
            denominator += weight
        home_ref[:, :, frame] = (numerator / denominator).astype(jnp.bfloat16)
    for distance in range(1, windows):
        target = lax.rem(here + distance, windows)
        first = first_owned(phase_of(owner_ref, target, windows), windows)
        if distance == windows - 1:
            left_ref[left_slots, :, :FROM_AFTER] = home_ref[:, :, :FROM_AFTER]
            for slot, index in enumerate(extra_owned(windows)):
                left_ref[left_slots, :, FROM_AFTER + slot] = home_ref[:, :, first + index * windows]
            continue
        sent_ref = sent_refs[distance - 1]
        for index in range(FR // windows):
            sent_ref[:, :, index] = home_ref[:, :, first + index * windows]
        if distance == 1:
            sent_ref[:, :, FR // windows :] = home_ref[:, :, FR - FROM_BEFORE :]


def place_body(windows, tables, in_refs, out_refs):
    place_ref, start_ref, owner_ref = tables[:3]
    home_ref, *received = in_refs
    owned_ref, next_ref, other_ref = out_refs
    here = place_ref[0]
    first = first_owned(phase_of(owner_ref, here, windows), windows)
    slot_base = (first + HOME_BASE) // windows
    count = FR // windows
    extra = extra_owned(windows)
    heads, _, _, _, head_size = home_ref.shape
    offset = start_ref[here] - here * FR + SHIFT - HOME_BASE
    from_before, from_after = received[0], received[-1]
    for head in range(heads):
        columns = slice(head * head_size, (head + 1) * head_size)
        for distance in range(windows):
            source = lax.rem(here + windows - distance, windows)
            for index in range(count):
                slot = lax.rem(source * count + slot_base + index, FR)
                if distance == 0:
                    row = home_ref[head, :, first + index * windows]
                elif distance < windows - 1:
                    row = received[distance - 1][head, :, index]
                elif index in extra:
                    row = received[distance - 1][head, :, FROM_AFTER + extra.index(index)]
                else:
                    row = received[distance - 1][head, :, first + index * windows]
                owned_ref[slot, :, columns] = row[0]
                other_ref[slot, :, columns] = row[1]
        for frame in range(WF):
            wanted = offset + frame
            row = home_ref[head, :, jnp.clip(wanted, 0, FR - 1)]
            if frame < FROM_BEFORE:
                slot = jnp.clip(wanted + FROM_BEFORE, 0, FROM_BEFORE - 1)
                row = jnp.where(wanted < 0, from_before[head, :, count + slot], row)
            if frame + MARGIN + SHIFT - HOME_BASE >= FR:
                slot = jnp.clip(wanted - FR, 0, FROM_AFTER - 1)
                row = jnp.where(wanted >= FR, from_after[head, :, slot], row)
            next_ref[frame, :, columns] = row[0]
            other_ref[FR + frame, :, columns] = row[1]


def block_spec(array, blocks, base=0):
    shape = (STEP_HEADS,) + array.shape[1:]
    zeros = (0,) * (len(shape) - 1)
    return pl.BlockSpec(
        shape, lambda i: (base // STEP_HEADS + jnp.minimum(i, blocks - 1),) + zeros
    )


class Task:
    def __init__(self, blocks, operands, in_specs, out_shape, out_specs, body):
        self.blocks, self.body = blocks, body
        self.operands, self.in_specs = operands, in_specs
        self.out_shape, self.out_specs = out_shape, out_specs


def attention_task(queries, sources):
    heads = sources[0].shape[0]
    blocks = heads // STEP_HEADS
    frames, tokens, head_size = queries[0][0].shape[1:]
    shape = like(heads, NEAR, frames, tokens, head_size)
    return Task(
        blocks,
        [query for query, _ in queries] + sources,
        [block_spec(query, blocks, base) for query, base in queries]
        + [block_spec(source, blocks) for source in sources],
        [shape],
        [block_spec(shape, blocks)],
        attention_body,
    )


def blend_task(out, after, after_base, windows):
    heads, halves, _, tokens, head_size = out.shape
    blocks = heads // STEP_HEADS
    owned = FR // windows
    counts = [FR, owned + FROM_BEFORE] + [owned] * (windows - 3)
    shapes = [like(heads, halves, count, tokens, head_size) for count in counts]
    return Task(
        blocks,
        [out, after],
        [block_spec(out, blocks), block_spec(after, blocks, after_base)],
        shapes,
        [block_spec(shape, blocks) for shape in shapes],
        functools.partial(blend_body, windows),
    )


def run_stage(tables, tasks, weight, merged=True):
    steps = max(task.blocks for task in tasks)
    operands = [operand for task in tasks for operand in task.operands]
    shapes = [shape for task in tasks for shape in task.out_shape]
    windows = lax.axis_size("win")
    assert left_count(windows) == HOME_BASE
    _, halves, _, tokens, head_size = shapes[0].shape
    blocks = [task.blocks * STEP_HEADS for task in tasks]
    lefts = [
        like(count, halves, HOME_BASE, tokens, head_size)
        for count in ([sum(blocks)] if merged else blocks)
    ]

    def kernel(*refs):
        table_refs, refs = refs[: len(tables)], refs[len(tables) :]
        in_refs, refs = refs[: len(operands)], refs[len(operands) :]
        out_refs, left_refs = refs[: len(shapes)], refs[len(shapes) :]
        step = pl.program_id(0)
        for index, task in enumerate(tasks):
            task_in, in_refs = in_refs[: len(task.operands)], in_refs[len(task.operands) :]
            task_out, out_refs = out_refs[: len(task.out_shape)], out_refs[len(task.out_shape) :]
            body = functools.partial(
                task.body,
                table_refs,
                task_in,
                task_out,
                left_refs[0 if merged else index],
                sum(blocks[:index]) if merged else 0,
            )
            if task.blocks == steps:
                body()
            else:
                pl.when(step < task.blocks)(body)

    outputs = pl.pallas_call(
        kernel,
        grid=(steps,),
        in_specs=[SMEM for _ in tables] + [spec for task in tasks for spec in task.in_specs],
        out_specs=[spec for task in tasks for spec in task.out_specs]
        + [pl.BlockSpec(left.shape, lambda i: (0,) * 5) for left in lefts],
        out_shape=shapes + lefts,
        compiler_params=params(),
        cost_estimate=cost(weight),
        name="stage",
    )(*tables, *operands)
    results = []
    for task in tasks:
        results.append(outputs[: len(task.out_shape)])
        outputs = outputs[len(task.out_shape) :]
    return results, outputs


def result_columns(half, base, width):
    head_size = width[1]
    column = (half * (HEADS // NEAR) + base) * head_size
    return pl.ds(pl.multiple_of(column, head_size), width[0] * head_size)


def place(tables, home, received, base, features, windows, targets, other, other_base, other_heads, weight):
    heads, halves, _, tokens, head_size = home.shape
    operands = [home, *received]
    earlier = [*targets, *([] if other is None else [other])]
    slots = ([0, 1] if targets else []) + ([] if other is None else [2])

    def first_heads(operand):
        return pl.BlockSpec((heads,) + operand.shape[1:], lambda i: (0,) * len(operand.shape))

    def kernel(*refs):
        table_refs, refs = refs[: len(tables)], refs[len(tables) :]
        in_refs, refs = refs[: len(operands)], refs[len(operands) + len(earlier) :]
        owned_ref, next_ref, other_ref, owned_rows, next_rows, other_rows, sems = refs
        place_body(windows, table_refs, in_refs, (owned_rows, next_rows, other_rows))
        columns = result_columns(table_refs[-1][0], base, (heads, head_size))
        other_columns = pl.ds(other_base * head_size, heads * head_size)
        copies = [
            pltpu.make_async_copy(other_rows, other_ref.at[:, :, other_columns], sems.at[2]),
            pltpu.make_async_copy(owned_rows, owned_ref.at[:, :, columns], sems.at[0]),
            pltpu.make_async_copy(next_rows, next_ref.at[:, :, columns], sems.at[1]),
        ]
        for copy in copies:
            copy.start()
        for copy in copies:
            copy.wait()

    anywhere = pl.BlockSpec(memory_space=pl.ANY)
    *targets, other = pl.pallas_call(
        kernel,
        grid=(1,),
        in_specs=[SMEM for _ in tables]
        + [first_heads(operand) for operand in operands]
        + [anywhere for _ in earlier],
        out_specs=[anywhere] * 3,
        out_shape=[
            like(FR, tokens, features),
            like(WF, tokens, features),
            like(FR + WF, tokens, other_heads * head_size),
        ],
        scratch_shapes=[
            pltpu.VMEM((FR, tokens, heads * head_size), jnp.bfloat16),
            pltpu.VMEM((WF, tokens, heads * head_size), jnp.bfloat16),
            pltpu.VMEM((FR + WF, tokens, heads * head_size), jnp.bfloat16),
            pltpu.SemaphoreType.DMA((3,)),
        ],
        input_output_aliases={
            len(tables) + len(operands) + i: slot for i, slot in enumerate(slots)
        },
        compiler_params=params(),
        cost_estimate=cost(weight),
        name="place",
    )(*tables, *operands, *earlier)
    return targets, other


def finish(near, others, bases, head_size, targets):
    def kernel(near_ref, *refs):
        in_refs, (owned_ref, next_ref, sems) = refs[: len(others)], refs[len(others) + 2 :]
        copies = []
        for index, (other_ref, base) in enumerate(zip(in_refs, bases)):
            heads = other_ref.shape[-1] // head_size
            columns = result_columns(NEAR - 1 - near_ref[0], base, (heads, head_size))
            copies += [
                pltpu.make_async_copy(
                    other_ref.at[pl.ds(0, FR)], owned_ref.at[:, :, columns], sems.at[2 * index]
                ),
                pltpu.make_async_copy(
                    other_ref.at[pl.ds(FR, WF)], next_ref.at[:, :, columns], sems.at[2 * index + 1]
                ),
            ]
        for copy in copies:
            copy.start()
        for copy in copies:
            copy.wait()

    anywhere = pl.BlockSpec(memory_space=pl.ANY)
    return pl.pallas_call(
        kernel,
        grid=(1,),
        in_specs=[SMEM]
        + [pl.BlockSpec(other.shape, lambda i: (0, 0, 0)) for other in others]
        + [anywhere for _ in targets],
        out_specs=[anywhere, anywhere],
        out_shape=[like(*target.shape) for target in targets],
        scratch_shapes=[pltpu.SemaphoreType.DMA((2 * len(others),))],
        input_output_aliases={1 + len(others) + i: i for i in range(2)},
        compiler_params=params(),
        cost_estimate=cost(TAIL_COST),
        name="finish",
    )(near, *others, *targets)


def exchange(array, bit):
    return lax.ppermute(array, "uly", [(i, i ^ bit) for i in range(lax.axis_size("uly"))])


def shift(array, step):
    count = lax.axis_size("win")
    return lax.ppermute(array, "win", [(i, (i + step) % count) for i in range(count)])


def after(array, *others):
    return lax.optimization_barrier((array, *others))[0] if others else array


def normalize(row_block, gain_vector):
    floats = row_block.astype(jnp.float32)
    mean_square = jnp.mean(floats * floats, axis=-1, keepdims=True)
    return (floats * lax.rsqrt(mean_square + 1e-06) * gain_vector).astype(jnp.bfloat16)


def head_attention(operands):
    query_head, key_head, value_head = operands
    scores = jnp.dot(query_head, key_head.T, preferred_element_type=jnp.float32) * (
        1.0 / math.sqrt(query_head.shape[-1])
    )
    row_max = jnp.max(scores, axis=-1, keepdims=True)
    exponent = jnp.exp(scores - row_max)
    weights = (exponent / jnp.sum(exponent, axis=-1, keepdims=True)).astype(jnp.bfloat16)
    return jnp.dot(weights, value_head, preferred_element_type=jnp.float32).astype(jnp.bfloat16)


def attend(operands):
    query_part, key_part, value_part = operands
    heads_here = query_part.shape[3]
    head_size = query_part.shape[4]
    token_count = query_part.shape[0] * query_part.shape[1]

    def flatten(tensor):
        return jnp.moveaxis(tensor.reshape(token_count, heads_here, head_size), 1, 0)

    result = lax.map(head_attention, (flatten(query_part), flatten(key_part), flatten(value_part)))
    return jnp.moveaxis(result, 0, 1).reshape(query_part.shape)


def table_lookup(table_row, wanted, length):
    entries = jnp.arange(length, dtype=jnp.int32)
    return jnp.sum(jnp.where(wanted[..., None] == entries, table_row, 0), axis=-1)


def send_owners(frame_rows, inverse, my_start, windows, capacity):
    slot_index = jnp.arange(capacity, dtype=jnp.int32)
    position_in = (inverse[:, None] - my_start) % windows + slot_index[None, :] * windows
    is_valid = (position_in < WF).reshape(-1)
    picked = jnp.take(frame_rows, jnp.minimum(position_in, WF - 1).reshape(-1), axis=0)
    picked = jnp.where(is_valid[:, None, None], picked, jnp.zeros_like(picked))
    packed = picked.reshape(windows, capacity, frame_rows.shape[1], frame_rows.shape[2])
    return lax.all_to_all(packed, "win", split_axis=0, concat_axis=0, tiled=True)


def combine_owned(received, window_start, blend_weight, my_phase, windows, frames_total, capacity):
    slot_index = jnp.arange(capacity, dtype=jnp.int32)
    source_pos = (my_phase - window_start[:, None]) % windows + slot_index[None, :] * windows
    arrived = source_pos < WF
    slot_at = (window_start[:, None] + source_pos) % frames_total // windows
    factor = table_lookup(blend_weight[:, None, :], source_pos, WF)
    owned_range = jnp.arange(FR, dtype=jnp.int32)
    mixing = jnp.where(
        (slot_at[None] == owned_range[:, None, None]) & arrived[None], factor[None], 0
    )
    mixing = mixing.reshape(FR, windows * capacity).astype(jnp.float32)
    numerator = jnp.dot(
        mixing.astype(jnp.bfloat16),
        received.reshape(windows * capacity, -1),
        preferred_element_type=jnp.float32,
    )
    denominator = jnp.sum(mixing, axis=1)
    owned = (numerator / denominator[:, None]).astype(jnp.bfloat16)
    return owned.reshape(FR, received.shape[2], received.shape[3])


def general(
    query_rows,
    key_rows,
    value_rows,
    query_gain,
    key_gain,
    window_start,
    owner_of_phase,
    blend_weight,
):
    windows = lax.axis_size("win")
    ulysses = lax.axis_size("uly")
    position = lax.axis_index("win")
    frames_total = FR * windows
    capacity = (WF + windows - 1) // windows
    shift_frames = FR // 2
    local_tokens = query_rows.shape[2]
    feature_count = query_rows.shape[3]
    groups = HEADS // ulysses
    head_size = feature_count // HEADS
    split_shape = (WF, local_tokens, ulysses, groups, head_size)
    query_heads = normalize(query_rows[0], query_gain).reshape(split_shape)
    key_heads = normalize(key_rows[0], key_gain).reshape(split_shape)
    value_heads = value_rows[0].reshape(split_shape)
    attended = attend(
        (
            lax.all_to_all(query_heads, "uly", split_axis=2, concat_axis=1, tiled=True),
            lax.all_to_all(key_heads, "uly", split_axis=2, concat_axis=1, tiled=True),
            lax.all_to_all(value_heads, "uly", split_axis=2, concat_axis=1, tiled=True),
        )
    )
    own_out = lax.all_to_all(attended, "uly", split_axis=1, concat_axis=2, tiled=True).reshape(
        WF, local_tokens, feature_count
    )
    phases = jnp.arange(windows, dtype=jnp.int32)
    inverse = jnp.sum(
        jnp.where(owner_of_phase[None, :] == phases[:, None], phases[None, :], 0), axis=1
    )
    my_start = window_start[position]
    my_phase = inverse[position]
    frame_range = jnp.arange(WF, dtype=jnp.int32)
    received = send_owners(own_out, inverse, my_start, windows, capacity)
    owned = combine_owned(
        received, window_start, blend_weight, my_phase, windows, frames_total, capacity
    )
    slot_index = jnp.arange(capacity, dtype=jnp.int32)
    target_pos = (my_phase - window_start[:, None] - shift_frames) % windows + slot_index[
        None, :
    ] * windows
    target_valid = (target_pos < WF).reshape(-1)
    target_slot = (
        (window_start[:, None] + shift_frames + target_pos) % frames_total // windows
    ).reshape(-1)
    outgoing = jnp.take(owned, target_slot, axis=0)
    outgoing = jnp.where(target_valid[:, None, None], outgoing, jnp.zeros_like(outgoing))
    outgoing = outgoing.reshape(windows, capacity, local_tokens, feature_count)
    returned = lax.all_to_all(outgoing, "win", split_axis=0, concat_axis=0, tiled=True)
    needed_phase = (my_start + shift_frames + frame_range) % windows
    source_owner = table_lookup(owner_of_phase[None, :], needed_phase, windows)
    flat_index = source_owner * capacity + frame_range // windows
    next_rows = jnp.take(
        returned.reshape(windows * capacity, local_tokens, feature_count), flat_index, axis=0
    )
    return (owned, next_rows[None])


def far_blocks(own):
    blocks = [own]
    bit = lax.axis_size("uly") // 2
    while bit >= NEAR:
        blocks += [exchange(block, bit) for block in blocks]
        bit //= 2
    return blocks


def pipelined(
    query_rows,
    key_rows,
    value_rows,
    query_gain,
    key_gain,
    window_start,
    owner_of_phase,
    blend_weight,
):
    windows = lax.axis_size("win")
    features = query_rows.shape[-1]
    head_size = features // HEADS
    near = lax.rem(lax.axis_index("uly"), NEAR).astype(jnp.int32).reshape(1)
    position = lax.axis_index("win").astype(jnp.int32).reshape(1)
    tables = (position, window_start, owner_of_phase, blend_weight, near)
    query_gain = query_gain.reshape(1, 1, features)
    key_gain = key_gain.reshape(1, 1, features)
    count = len(CHUNKS)
    bases = [sum(CHUNKS[:i]) for i in range(count)]

    groups = [CHUNKS[:1], CHUNKS[1:2], CHUNKS[2:]]
    own, *sent = split_heads(
        near, key_rows[0], key_gain, [sum(group) for group in groups], (value_rows[0],)
    )
    chunks, sources = [], {}

    def join_group(index, *earlier):
        other = exchange(after(sent[index], *chunks[:1]), 1)
        chunks.extend(
            join_halves(own, bases[len(chunks)], after(other, *earlier), groups[index])
        )

    join_group(0)
    sources[0] = far_blocks(chunks[0])
    own_queries, *sent_queries = split_heads(
        near, after(query_rows[0], chunks[0]), query_gain, [CHUNKS[0], sum(CHUNKS[1:])]
    )
    first_queries, later_queries = [exchange(array, 1) for array in sent_queries]
    join_group(1, own_queries)
    sources[1] = far_blocks(chunks[1])

    attended, homes, received, others = {}, {}, {}, {}
    targets = ()

    def shift_around(arrays, *earlier):
        return [
            shift(after(array, *earlier), distance) for distance, array in enumerate(arrays, 1)
        ]

    early = count - LATE_CHUNKS
    early_heads = sum(CHUNKS[:early])

    def place_chunk(chunk, *earlier):
        late = chunk >= early
        targets_now, others[late] = place(
            tables,
            after(homes[chunk], *earlier),
            received[chunk],
            bases[chunk],
            features,
            windows,
            targets,
            others.get(late),
            bases[chunk] - early_heads if late else bases[chunk],
            sum(CHUNKS) - early_heads if late else early_heads,
            TAIL_COST if chunk >= count - FREE else PLACE_COST,
        )
        return targets_now

    arrived, waiting = {}, {}

    def attend(chunk, *earlier):
        queries = (after(own_queries, *earlier), bases[chunk]), (
            (later_queries, bases[chunk] - bases[1]) if chunk else (first_queries, 0)
        )
        (((attended[chunk],),), (left,)) = run_stage(
            tables, [attention_task(queries, sources[chunk])], STAGE_COST
        )
        return left

    def mix(chunk, earlier, gate=()):
        ready = after(arrived[chunk], *earlier)
        (((homes[chunk], *waiting[chunk]),), (left,)) = run_stage(
            tables, [blend_task(attended[chunk], ready, 0, windows)], BLEND_COST
        )
        received[chunk] = [shift(after(left, *gate), -1)]

    def send_around(chunk, gates):
        received[chunk] = [
            shift(after(array, *gate), distance)
            for distance, (array, gate) in enumerate(zip(waiting[chunk], gates), 1)
        ] + received[chunk]

    swapped = SWAP if count > 3 else 0
    for chunk in range(count - swapped):
        left = attend(chunk, homes[chunk - 1] if chunk else chunks[1])
        gate = received[chunk - 1] if chunk else []
        arrived[chunk] = shift(after(left, *gate), -1)
        if chunk >= 1:
            send_around(chunk - 1, [[attended[chunk]]] * windows)
        if chunk >= 2:
            targets = place_chunk(chunk - 2, attended[chunk])
        if chunk == count - 1 - swapped and swapped:
            break
        mix(chunk, targets[:1])
        if chunk == 0:
            join_group(2, homes[0])
            for later in range(2, count):
                sources[later] = far_blocks(chunks[later])
    if swapped:
        left = attend(count - 1, attended[count - 2], targets[0])
        arrived[count - 1] = shift(left, -1)
        mix(count - 2, [attended[count - 1]])
        send_around(count - 2, [[]] * windows)
        if P3_TIE == 0:
            targets = place_chunk(count - 3, homes[count - 2])
        mix(count - 1, [homes[count - 2]], received[count - 2][-1:] if CHAIN else [])
    chained = CHAIN and swapped
    gates = [[array] for array in received[count - 2]] if chained else [[]] * windows
    send_around(count - 1, gates)
    if swapped and P3_TIE:
        targets = place_chunk(count - 3, homes[count - 1])
    targets = place_chunk(count - 2, homes[count - 1])
    if LATE_CHUNKS > 1:
        tie = (homes[count - 1], attended[count - 1], homes[count - 2])[OX_TIE]
        arrived = exchange(after(others[False], tie), 1)
    else:
        arrived = exchange(others[False], 1)
    targets = finish(near, [arrived], [0], head_size, targets)
    targets = place_chunk(count - 1)
    owned, next_rows = finish(
        near, [exchange(others[True], 1)], [early_heads], head_size, targets
    )
    return (owned, next_rows[None])


def per_device(*operands):
    windows, ulysses = lax.axis_size("win"), lax.axis_size("uly")
    fits = windows >= 3 and FR % windows == 0 and left_count(windows) == HOME_BASE
    if fits and ulysses >= NEAR and ulysses & (ulysses - 1) == 0:
        return pipelined(*operands)
    return general(*operands)


def solution(mesh):
    placed = (
        P(("grp", "win"), None, "uly", None),
        P(("grp", "win"), None, "uly", None),
        P(("grp", "win"), None, "uly", None),
        P(),
        P(),
        P("grp"),
        P("grp"),
        P("grp", None),
    )
    return jax.shard_map(
        per_device,
        mesh=mesh,
        in_specs=placed,
        out_specs=(P(("grp", "win"), "uly", None), P(("grp", "win"), None, "uly", None)),
        check_vma=False,
    )
```

```python
import functools
import math

import jax
import jax.numpy as jnp
from jax import lax
from jax.experimental import pallas as pl
from jax.experimental.pallas import tpu as pltpu
from jax.sharding import PartitionSpec as P

HEADS = 40
WF = 16
FR = 12
MARGIN = WF - FR
SHIFT = FR // 2
HOME_BASE = 2 * MARGIN
FROM_BEFORE = HOME_BASE - SHIFT
FROM_AFTER = SHIFT + WF + MARGIN - HOME_BASE - FR
NEAR = 2
CHUNKS = (2, 4, 4, 4, 4, 2)
STEP_HEADS = 2
VMEM_LIMIT = 64 * 1024 * 1024


def params():
    return pltpu.CompilerParams(vmem_limit_bytes=VMEM_LIMIT)


def like(*shape):
    return jax.ShapeDtypeStruct(shape, jnp.bfloat16)


def cost(microseconds):
    return pl.CostEstimate(
        flops=int(microseconds * 1.15e9), bytes_accessed=0, transcendentals=0
    )


NORM_COST = 8.7
JOIN_COST = 8.7
REST_COST = 0.0
STAGE_COST = 0.0
BLEND_COST = 0.0
SWAP = 1
PLACE_COST = 7.5
TAIL_COST = 1.5
LATE_CHUNKS = 1
FREE = 1
P3_TIE = 0
CHAIN = 1
OX_TIE = 0
SMEM = pl.BlockSpec(memory_space=pltpu.SMEM)


def split_heads(near, rows, gain, counts, plain=(), frames_per_step=8):
    frames, tokens, features = rows.shape
    head_size = features // HEADS
    kinds = (2,) * len(plain)
    heads = HEADS // NEAR

    def kernel(near_ref, rows_ref, gain_ref, *refs):
        plain_refs, out_refs = refs[: len(plain)], refs[len(plain) :]
        here = near_ref[0]
        squares = jnp.zeros((frames_per_step, tokens, head_size), jnp.float32)
        for head in range(HEADS):
            floats = rows_ref[:, :, head * head_size : (head + 1) * head_size].astype(jnp.float32)
            squares += floats * floats
        mean_square = jnp.sum(squares, axis=-1, keepdims=True) / features
        scale = jnp.broadcast_to(lax.rsqrt(mean_square + 1e-06), squares.shape)

        def put(out_ref, slot, half, head):
            column = pl.multiple_of((half * heads + head) * head_size, head_size)
            columns = pl.ds(column, head_size)
            floats = rows_ref[:, :, columns].astype(jnp.float32)
            normalized = (floats * scale * gain_ref[:, :, columns]).astype(jnp.bfloat16)
            if plain:
                out_ref[slot, 0] = normalized
                out_ref[slot, 1] = plain_refs[0][:, :, columns]
            else:
                out_ref[slot] = normalized

        for head in range(heads):
            put(out_refs[0], head, here, head)
        head = 0
        for out_ref in out_refs[1:]:
            for slot in range(out_ref.shape[0]):
                put(out_ref, slot, NEAR - 1 - here, head)
                head += 1

    block = pl.BlockSpec((frames_per_step, tokens, features), lambda i: (i, 0, 0))

    def out_spec(count):
        zeros = (0,) * (1 + len(kinds))
        return pl.BlockSpec(
            (count, *kinds, frames_per_step, tokens, head_size), lambda i: (*zeros, i, 0, 0)
        )

    return pl.pallas_call(
        kernel,
        grid=(frames // frames_per_step,),
        in_specs=[SMEM, block, pl.BlockSpec((1, 1, features), lambda i: (0, 0, 0))]
        + [block for _ in plain],
        out_specs=[out_spec(count) for count in (sum(counts), *counts)],
        out_shape=[
            like(count, *kinds, frames, tokens, head_size) for count in (sum(counts), *counts)
        ],
        compiler_params=params(),
        cost_estimate=cost(NORM_COST),
        name="norm_split",
    )(near, rows, gain, *plain)


def join_halves(own, base, other, counts):
    _, kinds, frames, tokens, head_size = own.shape
    bases = [sum(counts[:i]) for i in range(len(counts))]

    def out_spec(first, count):
        return pl.BlockSpec(
            (STEP_HEADS, kinds, NEAR, frames, tokens, head_size),
            lambda i: (jnp.clip(i - first // STEP_HEADS, 0, count // STEP_HEADS - 1),) + (0,) * 5,
        )

    def kernel(own_ref, other_ref, *out_refs):
        step = pl.program_id(0) * STEP_HEADS
        for out_ref, first, count in zip(out_refs, bases, counts):

            @pl.when((step >= first) & (step < first + count))
            def _():
                out_ref[:, :, 0] = own_ref[...]
                out_ref[:, :, 1] = other_ref[...]

    block = (STEP_HEADS, kinds, frames, tokens, head_size)
    return pl.pallas_call(
        kernel,
        grid=(sum(counts) // STEP_HEADS,),
        in_specs=[
            pl.BlockSpec(block, lambda i: (base // STEP_HEADS + i, 0, 0, 0, 0)),
            pl.BlockSpec(block, lambda i: (i, 0, 0, 0, 0)),
        ],
        out_specs=[out_spec(first, count) for first, count in zip(bases, counts)],
        out_shape=[
            like(count, kinds, NEAR, frames, tokens, head_size) for count in counts
        ],
        compiler_params=params(),
        cost_estimate=cost(JOIN_COST if len(counts) == 1 else REST_COST),
        name="join_halves",
    )(own, other)


def attention_body(tables, in_refs, out_refs, left_ref, left_base):
    query_refs, sources = in_refs[:NEAR], in_refs[NEAR:]
    (out_ref,) = out_refs
    _, frames, tokens, head_size = query_refs[0].shape
    rows = frames * tokens
    factor = math.log2(math.e) / math.sqrt(head_size)
    contract = (((1,), (1,)), ((), ()))
    left_slot = left_base + pl.program_id(0) * STEP_HEADS

    def scores_of(head, half):
        query = query_refs[half][head].reshape(rows, head_size)
        return [
            lax.dot_general(
                query,
                source[head, 0].reshape(NEAR * rows, head_size),
                contract,
                preferred_element_type=jnp.float32,
            )
            for source in sources
        ]

    pieces = [(head, half) for head in range(STEP_HEADS) for half in range(NEAR)]
    following = scores_of(*pieces[0])
    for index, (head, half) in enumerate(pieces):
        scores = following
        if index + 1 < len(pieces):
            following = scores_of(*pieces[index + 1])
        row_max = functools.reduce(jnp.maximum, scores)
        row_max = jnp.max(row_max, axis=-1, keepdims=True)
        exponents = [jnp.exp2((score - row_max) * factor) for score in scores]
        total = jnp.sum(functools.reduce(jnp.add, exponents), axis=-1, keepdims=True)
        inverse = 1.0 / total
        result = jnp.zeros((rows, head_size), jnp.float32)
        for exponent, source in zip(exponents, sources):
            weights = (exponent * inverse).astype(jnp.bfloat16)
            result += jnp.dot(
                weights,
                source[head, 1].reshape(NEAR * rows, head_size),
                preferred_element_type=jnp.float32,
            )
        result = result.astype(jnp.bfloat16).reshape(frames, tokens, head_size)
        out_ref[head, half] = result
        left_ref[left_slot + head, half] = result[:HOME_BASE]


def phase_of(owner_ref, wanted, windows):
    phase = jnp.int32(0)
    for index in range(windows):
        phase = jnp.where(owner_ref[index] == wanted, index, phase)
    return phase


def first_owned(phase, windows):
    return lax.rem(phase + (windows - 1) * HOME_BASE, windows)


def extra_owned(windows):
    return [i for i in range(FR // windows) if windows * (i + 1) > FROM_AFTER]


def left_count(windows):
    return FROM_AFTER + len(extra_owned(windows))


def blend_body(windows, tables, in_refs, out_refs, left_ref, left_base):
    place_ref, start_ref, owner_ref, weight_ref, _ = tables
    out_ref, after_ref = in_refs
    home_ref, *sent_refs = out_refs
    here = place_ref[0]
    after = lax.rem(here + 1, windows)
    offset = start_ref[here] - here * FR
    offset_after = start_ref[after] - after * FR
    left_slots = pl.ds(left_base + pl.program_id(0) * STEP_HEADS, STEP_HEADS)
    for frame in range(FR):
        place = frame + HOME_BASE - offset
        if frame + HOME_BASE < WF:
            weight = weight_ref[here, place].astype(jnp.float32)
        else:
            valid = place < WF
            place = jnp.minimum(place, WF - 1)
            weight = jnp.where(valid, weight_ref[here, place], 0).astype(jnp.float32)
        numerator = out_ref[:, :, place].astype(jnp.float32) * weight
        denominator = weight
        if frame + HOME_BASE >= FR:
            slot = frame + HOME_BASE - FR - offset_after
            valid = slot >= 0
            slot = jnp.maximum(slot, 0)
            weight = jnp.where(valid, weight_ref[after, slot], 0).astype(jnp.float32)
            numerator += after_ref[:, :, slot].astype(jnp.float32) * weight
            denominator += weight
        home_ref[:, :, frame] = (numerator / denominator).astype(jnp.bfloat16)
    for distance in range(1, windows):
        target = lax.rem(here + distance, windows)
        first = first_owned(phase_of(owner_ref, target, windows), windows)
        if distance == windows - 1:
            left_ref[left_slots, :, :FROM_AFTER] = home_ref[:, :, :FROM_AFTER]
            for slot, index in enumerate(extra_owned(windows)):
                left_ref[left_slots, :, FROM_AFTER + slot] = home_ref[:, :, first + index * windows]
            continue
        sent_ref = sent_refs[distance - 1]
        for index in range(FR // windows):
            sent_ref[:, :, index] = home_ref[:, :, first + index * windows]
        if distance == 1:
            sent_ref[:, :, FR // windows :] = home_ref[:, :, FR - FROM_BEFORE :]


def place_body(windows, tables, in_refs, out_refs):
    place_ref, start_ref, owner_ref = tables[:3]
    home_ref, *received = in_refs
    owned_ref, next_ref, other_ref = out_refs
    here = place_ref[0]
    first = first_owned(phase_of(owner_ref, here, windows), windows)
    slot_base = (first + HOME_BASE) // windows
    count = FR // windows
    extra = extra_owned(windows)
    heads, _, _, _, head_size = home_ref.shape
    offset = start_ref[here] - here * FR + SHIFT - HOME_BASE
    from_before, from_after = received[0], received[-1]
    for head in range(heads):
        columns = slice(head * head_size, (head + 1) * head_size)
        for distance in range(windows):
            source = lax.rem(here + windows - distance, windows)
            for index in range(count):
                slot = lax.rem(source * count + slot_base + index, FR)
                if distance == 0:
                    row = home_ref[head, :, first + index * windows]
                elif distance < windows - 1:
                    row = received[distance - 1][head, :, index]
                elif index in extra:
                    row = received[distance - 1][head, :, FROM_AFTER + extra.index(index)]
                else:
                    row = received[distance - 1][head, :, first + index * windows]
                owned_ref[slot, :, columns] = row[0]
                other_ref[slot, :, columns] = row[1]
        for frame in range(WF):
            wanted = offset + frame
            row = home_ref[head, :, jnp.clip(wanted, 0, FR - 1)]
            if frame < FROM_BEFORE:
                slot = jnp.clip(wanted + FROM_BEFORE, 0, FROM_BEFORE - 1)
                row = jnp.where(wanted < 0, from_before[head, :, count + slot], row)
            if frame + MARGIN + SHIFT - HOME_BASE >= FR:
                slot = jnp.clip(wanted - FR, 0, FROM_AFTER - 1)
                row = jnp.where(wanted >= FR, from_after[head, :, slot], row)
            next_ref[frame, :, columns] = row[0]
            other_ref[FR + frame, :, columns] = row[1]


def block_spec(array, blocks, base=0):
    shape = (STEP_HEADS,) + array.shape[1:]
    zeros = (0,) * (len(shape) - 1)
    return pl.BlockSpec(
        shape, lambda i: (base // STEP_HEADS + jnp.minimum(i, blocks - 1),) + zeros
    )


class Task:
    def __init__(self, blocks, operands, in_specs, out_shape, out_specs, body):
        self.blocks, self.body = blocks, body
        self.operands, self.in_specs = operands, in_specs
        self.out_shape, self.out_specs = out_shape, out_specs


def attention_task(queries, sources):
    heads = sources[0].shape[0]
    blocks = heads // STEP_HEADS
    frames, tokens, head_size = queries[0][0].shape[1:]
    shape = like(heads, NEAR, frames, tokens, head_size)
    return Task(
        blocks,
        [query for query, _ in queries] + sources,
        [block_spec(query, blocks, base) for query, base in queries]
        + [block_spec(source, blocks) for source in sources],
        [shape],
        [block_spec(shape, blocks)],
        attention_body,
    )


def blend_task(out, after, after_base, windows):
    heads, halves, _, tokens, head_size = out.shape
    blocks = heads // STEP_HEADS
    owned = FR // windows
    counts = [FR, owned + FROM_BEFORE] + [owned] * (windows - 3)
    shapes = [like(heads, halves, count, tokens, head_size) for count in counts]
    return Task(
        blocks,
        [out, after],
        [block_spec(out, blocks), block_spec(after, blocks, after_base)],
        shapes,
        [block_spec(shape, blocks) for shape in shapes],
        functools.partial(blend_body, windows),
    )


def run_stage(tables, tasks, weight, merged=True):
    steps = max(task.blocks for task in tasks)
    operands = [operand for task in tasks for operand in task.operands]
    shapes = [shape for task in tasks for shape in task.out_shape]
    windows = lax.axis_size("win")
    assert left_count(windows) == HOME_BASE
    _, halves, _, tokens, head_size = shapes[0].shape
    blocks = [task.blocks * STEP_HEADS for task in tasks]
    lefts = [
        like(count, halves, HOME_BASE, tokens, head_size)
        for count in ([sum(blocks)] if merged else blocks)
    ]

    def kernel(*refs):
        table_refs, refs = refs[: len(tables)], refs[len(tables) :]
        in_refs, refs = refs[: len(operands)], refs[len(operands) :]
        out_refs, left_refs = refs[: len(shapes)], refs[len(shapes) :]
        step = pl.program_id(0)
        for index, task in enumerate(tasks):
            task_in, in_refs = in_refs[: len(task.operands)], in_refs[len(task.operands) :]
            task_out, out_refs = out_refs[: len(task.out_shape)], out_refs[len(task.out_shape) :]
            body = functools.partial(
                task.body,
                table_refs,
                task_in,
                task_out,
                left_refs[0 if merged else index],
                sum(blocks[:index]) if merged else 0,
            )
            if task.blocks == steps:
                body()
            else:
                pl.when(step < task.blocks)(body)

    outputs = pl.pallas_call(
        kernel,
        grid=(steps,),
        in_specs=[SMEM for _ in tables] + [spec for task in tasks for spec in task.in_specs],
        out_specs=[spec for task in tasks for spec in task.out_specs]
        + [pl.BlockSpec(left.shape, lambda i: (0,) * 5) for left in lefts],
        out_shape=shapes + lefts,
        compiler_params=params(),
        cost_estimate=cost(weight),
        name="stage",
    )(*tables, *operands)
    results = []
    for task in tasks:
        results.append(outputs[: len(task.out_shape)])
        outputs = outputs[len(task.out_shape) :]
    return results, outputs


def result_columns(half, base, width):
    head_size = width[1]
    column = (half * (HEADS // NEAR) + base) * head_size
    return pl.ds(pl.multiple_of(column, head_size), width[0] * head_size)


def place(tables, home, received, base, features, windows, targets, other, other_base, other_heads, weight):
    heads, halves, _, tokens, head_size = home.shape
    operands = [home, *received]
    earlier = [*targets, *([] if other is None else [other])]
    slots = ([0, 1] if targets else []) + ([] if other is None else [2])

    def first_heads(operand):
        return pl.BlockSpec((heads,) + operand.shape[1:], lambda i: (0,) * len(operand.shape))

    def kernel(*refs):
        table_refs, refs = refs[: len(tables)], refs[len(tables) :]
        in_refs, refs = refs[: len(operands)], refs[len(operands) + len(earlier) :]
        owned_ref, next_ref, other_ref, owned_rows, next_rows, other_rows, sems = refs
        place_body(windows, table_refs, in_refs, (owned_rows, next_rows, other_rows))
        columns = result_columns(table_refs[-1][0], base, (heads, head_size))
        other_columns = pl.ds(other_base * head_size, heads * head_size)
        copies = [
            pltpu.make_async_copy(other_rows, other_ref.at[:, :, other_columns], sems.at[2]),
            pltpu.make_async_copy(owned_rows, owned_ref.at[:, :, columns], sems.at[0]),
            pltpu.make_async_copy(next_rows, next_ref.at[:, :, columns], sems.at[1]),
        ]
        for copy in copies:
            copy.start()
        for copy in copies:
            copy.wait()

    anywhere = pl.BlockSpec(memory_space=pl.ANY)
    *targets, other = pl.pallas_call(
        kernel,
        grid=(1,),
        in_specs=[SMEM for _ in tables]
        + [first_heads(operand) for operand in operands]
        + [anywhere for _ in earlier],
        out_specs=[anywhere] * 3,
        out_shape=[
            like(FR, tokens, features),
            like(WF, tokens, features),
            like(FR + WF, tokens, other_heads * head_size),
        ],
        scratch_shapes=[
            pltpu.VMEM((FR, tokens, heads * head_size), jnp.bfloat16),
            pltpu.VMEM((WF, tokens, heads * head_size), jnp.bfloat16),
            pltpu.VMEM((FR + WF, tokens, heads * head_size), jnp.bfloat16),
            pltpu.SemaphoreType.DMA((3,)),
        ],
        input_output_aliases={
            len(tables) + len(operands) + i: slot for i, slot in enumerate(slots)
        },
        compiler_params=params(),
        cost_estimate=cost(weight),
        name="place",
    )(*tables, *operands, *earlier)
    return targets, other


def finish(near, others, bases, head_size, targets):
    def kernel(near_ref, *refs):
        in_refs, (owned_ref, next_ref, sems) = refs[: len(others)], refs[len(others) + 2 :]
        copies = []
        for index, (other_ref, base) in enumerate(zip(in_refs, bases)):
            heads = other_ref.shape[-1] // head_size
            columns = result_columns(NEAR - 1 - near_ref[0], base, (heads, head_size))
            copies += [
                pltpu.make_async_copy(
                    other_ref.at[pl.ds(0, FR)], owned_ref.at[:, :, columns], sems.at[2 * index]
                ),
                pltpu.make_async_copy(
                    other_ref.at[pl.ds(FR, WF)], next_ref.at[:, :, columns], sems.at[2 * index + 1]
                ),
            ]
        for copy in copies:
            copy.start()
        for copy in copies:
            copy.wait()

    anywhere = pl.BlockSpec(memory_space=pl.ANY)
    return pl.pallas_call(
        kernel,
        grid=(1,),
        in_specs=[SMEM]
        + [pl.BlockSpec(other.shape, lambda i: (0, 0, 0)) for other in others]
        + [anywhere for _ in targets],
        out_specs=[anywhere, anywhere],
        out_shape=[like(*target.shape) for target in targets],
        scratch_shapes=[pltpu.SemaphoreType.DMA((2 * len(others),))],
        input_output_aliases={1 + len(others) + i: i for i in range(2)},
        compiler_params=params(),
        cost_estimate=cost(TAIL_COST),
        name="finish",
    )(near, *others, *targets)


def exchange(array, bit):
    return lax.ppermute(array, "uly", [(i, i ^ bit) for i in range(lax.axis_size("uly"))])


def shift(array, step):
    count = lax.axis_size("win")
    return lax.ppermute(array, "win", [(i, (i + step) % count) for i in range(count)])


def after(array, *others):
    return lax.optimization_barrier((array, *others))[0] if others else array


def normalize(row_block, gain_vector):
    floats = row_block.astype(jnp.float32)
    mean_square = jnp.mean(floats * floats, axis=-1, keepdims=True)
    return (floats * lax.rsqrt(mean_square + 1e-06) * gain_vector).astype(jnp.bfloat16)


def head_attention(operands):
    query_head, key_head, value_head = operands
    scores = jnp.dot(query_head, key_head.T, preferred_element_type=jnp.float32) * (
        1.0 / math.sqrt(query_head.shape[-1])
    )
    row_max = jnp.max(scores, axis=-1, keepdims=True)
    exponent = jnp.exp(scores - row_max)
    weights = (exponent / jnp.sum(exponent, axis=-1, keepdims=True)).astype(jnp.bfloat16)
    return jnp.dot(weights, value_head, preferred_element_type=jnp.float32).astype(jnp.bfloat16)


def attend(operands):
    query_part, key_part, value_part = operands
    heads_here = query_part.shape[3]
    head_size = query_part.shape[4]
    token_count = query_part.shape[0] * query_part.shape[1]

    def flatten(tensor):
        return jnp.moveaxis(tensor.reshape(token_count, heads_here, head_size), 1, 0)

    result = lax.map(head_attention, (flatten(query_part), flatten(key_part), flatten(value_part)))
    return jnp.moveaxis(result, 0, 1).reshape(query_part.shape)


def table_lookup(table_row, wanted, length):
    entries = jnp.arange(length, dtype=jnp.int32)
    return jnp.sum(jnp.where(wanted[..., None] == entries, table_row, 0), axis=-1)


def send_owners(frame_rows, inverse, my_start, windows, capacity):
    slot_index = jnp.arange(capacity, dtype=jnp.int32)
    position_in = (inverse[:, None] - my_start) % windows + slot_index[None, :] * windows
    is_valid = (position_in < WF).reshape(-1)
    picked = jnp.take(frame_rows, jnp.minimum(position_in, WF - 1).reshape(-1), axis=0)
    picked = jnp.where(is_valid[:, None, None], picked, jnp.zeros_like(picked))
    packed = picked.reshape(windows, capacity, frame_rows.shape[1], frame_rows.shape[2])
    return lax.all_to_all(packed, "win", split_axis=0, concat_axis=0, tiled=True)


def combine_owned(received, window_start, blend_weight, my_phase, windows, frames_total, capacity):
    slot_index = jnp.arange(capacity, dtype=jnp.int32)
    source_pos = (my_phase - window_start[:, None]) % windows + slot_index[None, :] * windows
    arrived = source_pos < WF
    slot_at = (window_start[:, None] + source_pos) % frames_total // windows
    factor = table_lookup(blend_weight[:, None, :], source_pos, WF)
    owned_range = jnp.arange(FR, dtype=jnp.int32)
    mixing = jnp.where(
        (slot_at[None] == owned_range[:, None, None]) & arrived[None], factor[None], 0
    )
    mixing = mixing.reshape(FR, windows * capacity).astype(jnp.float32)
    numerator = jnp.dot(
        mixing.astype(jnp.bfloat16),
        received.reshape(windows * capacity, -1),
        preferred_element_type=jnp.float32,
    )
    denominator = jnp.sum(mixing, axis=1)
    owned = (numerator / denominator[:, None]).astype(jnp.bfloat16)
    return owned.reshape(FR, received.shape[2], received.shape[3])


def general(
    query_rows,
    key_rows,
    value_rows,
    query_gain,
    key_gain,
    window_start,
    owner_of_phase,
    blend_weight,
):
    windows = lax.axis_size("win")
    ulysses = lax.axis_size("uly")
    position = lax.axis_index("win")
    frames_total = FR * windows
    capacity = (WF + windows - 1) // windows
    shift_frames = FR // 2
    local_tokens = query_rows.shape[2]
    feature_count = query_rows.shape[3]
    groups = HEADS // ulysses
    head_size = feature_count // HEADS
    split_shape = (WF, local_tokens, ulysses, groups, head_size)
    query_heads = normalize(query_rows[0], query_gain).reshape(split_shape)
    key_heads = normalize(key_rows[0], key_gain).reshape(split_shape)
    value_heads = value_rows[0].reshape(split_shape)
    attended = attend(
        (
            lax.all_to_all(query_heads, "uly", split_axis=2, concat_axis=1, tiled=True),
            lax.all_to_all(key_heads, "uly", split_axis=2, concat_axis=1, tiled=True),
            lax.all_to_all(value_heads, "uly", split_axis=2, concat_axis=1, tiled=True),
        )
    )
    own_out = lax.all_to_all(attended, "uly", split_axis=1, concat_axis=2, tiled=True).reshape(
        WF, local_tokens, feature_count
    )
    phases = jnp.arange(windows, dtype=jnp.int32)
    inverse = jnp.sum(
        jnp.where(owner_of_phase[None, :] == phases[:, None], phases[None, :], 0), axis=1
    )
    my_start = window_start[position]
    my_phase = inverse[position]
    frame_range = jnp.arange(WF, dtype=jnp.int32)
    received = send_owners(own_out, inverse, my_start, windows, capacity)
    owned = combine_owned(
        received, window_start, blend_weight, my_phase, windows, frames_total, capacity
    )
    slot_index = jnp.arange(capacity, dtype=jnp.int32)
    target_pos = (my_phase - window_start[:, None] - shift_frames) % windows + slot_index[
        None, :
    ] * windows
    target_valid = (target_pos < WF).reshape(-1)
    target_slot = (
        (window_start[:, None] + shift_frames + target_pos) % frames_total // windows
    ).reshape(-1)
    outgoing = jnp.take(owned, target_slot, axis=0)
    outgoing = jnp.where(target_valid[:, None, None], outgoing, jnp.zeros_like(outgoing))
    outgoing = outgoing.reshape(windows, capacity, local_tokens, feature_count)
    returned = lax.all_to_all(outgoing, "win", split_axis=0, concat_axis=0, tiled=True)
    needed_phase = (my_start + shift_frames + frame_range) % windows
    source_owner = table_lookup(owner_of_phase[None, :], needed_phase, windows)
    flat_index = source_owner * capacity + frame_range // windows
    next_rows = jnp.take(
        returned.reshape(windows * capacity, local_tokens, feature_count), flat_index, axis=0
    )
    return (owned, next_rows[None])


def far_blocks(own):
    blocks = [own]
    bit = lax.axis_size("uly") // 2
    while bit >= NEAR:
        blocks += [exchange(block, bit) for block in blocks]
        bit //= 2
    return blocks


def pipelined(
    query_rows,
    key_rows,
    value_rows,
    query_gain,
    key_gain,
    window_start,
    owner_of_phase,
    blend_weight,
):
    windows = lax.axis_size("win")
    features = query_rows.shape[-1]
    head_size = features // HEADS
    near = lax.rem(lax.axis_index("uly"), NEAR).astype(jnp.int32).reshape(1)
    position = lax.axis_index("win").astype(jnp.int32).reshape(1)
    tables = (position, window_start, owner_of_phase, blend_weight, near)
    query_gain = query_gain.reshape(1, 1, features)
    key_gain = key_gain.reshape(1, 1, features)
    count = len(CHUNKS)
    bases = [sum(CHUNKS[:i]) for i in range(count)]

    groups = [CHUNKS[:1], CHUNKS[1:2], CHUNKS[2:]]
    own, *sent = split_heads(
        near, key_rows[0], key_gain, [sum(group) for group in groups], (value_rows[0],)
    )
    chunks, sources = [], {}

    def join_group(index, *earlier):
        other = exchange(after(sent[index], *chunks[:1]), 1)
        chunks.extend(
            join_halves(own, bases[len(chunks)], after(other, *earlier), groups[index])
        )

    join_group(0)
    sources[0] = far_blocks(chunks[0])
    own_queries, *sent_queries = split_heads(
        near, after(query_rows[0], chunks[0]), query_gain, [CHUNKS[0], sum(CHUNKS[1:])]
    )
    first_queries, later_queries = [exchange(array, 1) for array in sent_queries]
    join_group(1, own_queries)
    sources[1] = far_blocks(chunks[1])

    attended, homes, received, others = {}, {}, {}, {}
    targets = ()

    def shift_around(arrays, *earlier):
        return [
            shift(after(array, *earlier), distance) for distance, array in enumerate(arrays, 1)
        ]

    early = count - LATE_CHUNKS
    early_heads = sum(CHUNKS[:early])

    def place_chunk(chunk, *earlier):
        late = chunk >= early
        targets_now, others[late] = place(
            tables,
            after(homes[chunk], *earlier),
            received[chunk],
            bases[chunk],
            features,
            windows,
            targets,
            others.get(late),
            bases[chunk] - early_heads if late else bases[chunk],
            sum(CHUNKS) - early_heads if late else early_heads,
            TAIL_COST if chunk >= count - FREE else PLACE_COST,
        )
        return targets_now

    arrived, waiting = {}, {}

    def attend(chunk, *earlier):
        queries = (after(own_queries, *earlier), bases[chunk]), (
            (later_queries, bases[chunk] - bases[1]) if chunk else (first_queries, 0)
        )
        (((attended[chunk],),), (left,)) = run_stage(
            tables, [attention_task(queries, sources[chunk])], STAGE_COST
        )
        return left

    def mix(chunk, earlier, gate=()):
        ready = after(arrived[chunk], *earlier)
        (((homes[chunk], *waiting[chunk]),), (left,)) = run_stage(
            tables, [blend_task(attended[chunk], ready, 0, windows)], BLEND_COST
        )
        received[chunk] = [shift(after(left, *gate), -1)]

    def send_around(chunk, gates):
        received[chunk] = [
            shift(after(array, *gate), distance)
            for distance, (array, gate) in enumerate(zip(waiting[chunk], gates), 1)
        ] + received[chunk]

    swapped = SWAP if count > 3 else 0
    for chunk in range(count - swapped):
        left = attend(chunk, homes[chunk - 1] if chunk else chunks[1])
        gate = received[chunk - 1] if chunk else []
        arrived[chunk] = shift(after(left, *gate), -1)
        if chunk >= 1:
            send_around(chunk - 1, [[attended[chunk]]] * windows)
        if chunk >= 2:
            targets = place_chunk(chunk - 2, attended[chunk])
        if chunk == count - 1 - swapped and swapped:
            break
        mix(chunk, targets[:1])
        if chunk == 0:
            join_group(2, homes[0])
            for later in range(2, count):
                sources[later] = far_blocks(chunks[later])
    if swapped:
        left = attend(count - 1, attended[count - 2], targets[0])
        arrived[count - 1] = shift(left, -1)
        mix(count - 2, [attended[count - 1]])
        send_around(count - 2, [[]] * windows)
        if P3_TIE == 0:
            targets = place_chunk(count - 3, homes[count - 2])
        mix(count - 1, [homes[count - 2]], received[count - 2][-1:] if CHAIN else [])
    chained = CHAIN and swapped
    gates = [[array] for array in received[count - 2]] if chained else [[]] * windows
    send_around(count - 1, gates)
    if swapped and P3_TIE:
        targets = place_chunk(count - 3, homes[count - 1])
    targets = place_chunk(count - 2, homes[count - 1])
    if LATE_CHUNKS > 1:
        tie = (homes[count - 1], attended[count - 1], homes[count - 2])[OX_TIE]
        arrived = exchange(after(others[False], tie), 1)
    else:
        arrived = exchange(others[False], 1)
    targets = finish(near, [arrived], [0], head_size, targets)
    targets = place_chunk(count - 1)
    owned, next_rows = finish(
        near, [exchange(others[True], 1)], [early_heads], head_size, targets
    )
    return (owned, next_rows[None])


def per_device(*operands):
    windows, ulysses = lax.axis_size("win"), lax.axis_size("uly")
    fits = windows >= 3 and FR % windows == 0 and left_count(windows) == HOME_BASE
    if fits and ulysses >= NEAR and ulysses & (ulysses - 1) == 0:
        return pipelined(*operands)
    return general(*operands)


def solution(mesh):
    placed = (
        P(("grp", "win"), None, "uly", None),
        P(("grp", "win"), None, "uly", None),
        P(("grp", "win"), None, "uly", None),
        P(),
        P(),
        P("grp"),
        P("grp"),
        P("grp", None),
    )
    return jax.shard_map(
        per_device,
        mesh=mesh,
        in_specs=placed,
        out_specs=(P(("grp", "win"), "uly", None), P(("grp", "win"), None, "uly", None)),
        check_vma=False,
    )
```
